256 devices in a mesh: section: 16 (over z, x_lo), expert: 16 (over y, x_hi, core).
Axes of the slice: x: 4 (x_hi: 2, x_lo: 2; x = x_hi * 2 + x_lo), y: 4, z: 8, core: 2. Of those that a mesh axis runs over, the one named last changes fastest.
Arguments:
- state: bfloat16 [16, 2048, 4096], P('section', 'expert'), may hold values from -6 to 6
- lengths: int32 [16], P('section'), may hold values from 128 to 2048, as said below
- gain: float32 [16, 4096], P('section'), may hold values from 0.25 to 1.75
- w_gate: bfloat16 [16, 4096, 6144], P('section', None, 'expert'), may hold values from -0.09375 to 0.09375
- w_up: bfloat16 [16, 4096, 6144], P('section', None, 'expert'), may hold values from -0.09375 to 0.09375
- w_down: bfloat16 [16, 6144, 4096], P('section', 'expert'), may hold values from -0.21875 to 0.21875
- expert_ids: int32 [2, 16, 2048, 2], P(None, 'section', 'expert'), may hold values from 0 to 7, all different within a row; in each aligned block of 128 rows (0 to 127, 128 to 255, ..., all dimensions but the last counted through in order) at most 40 rows name the same one
- gate_weights: float32 [2, 16, 2048, 2], P(None, 'section', 'expert'), may hold values from 0.1 to 1
Outputs:
- hidden_out: bfloat16 [16, 2048, 4096], P('section', 'expert')
The draws below stay inside these ranges and needn't reach their ends.
Inputs may be any that keep to these rules, and one draw needn't show every extreme that they name: `expert_ids`: in each aligned block of 128 rows (the rows of one device) no expert is named by more than 40 rows, a bound that some block reaches; a row names 2 different experts. `lengths`: live rows are a prefix of each micro-batch; the micro-batch at section 0 is full.
All inputs are finite; a program needn't handle non-finite values.
Results may differ from the reference program's by a relative error of at most 0.0059.
Values may be sent and summed in bfloat16 or wider, within the bound.
A program may use at most 128 MiB of HBM per device.

```python
import math
import jax
import jax.numpy as jnp
import numpy as np
from jax import lax

D = 4096
FFW = 768
TOP = 2
STEPS = 2
TOK_DEV = 128
LAYERS = 16
EXPERTS = 8
TOKENS_G = 2048
CAP = 40
N_EXPERT = 16


def draw_lengths(key, part):
    key = jax.random.fold_in(key, 7)
    drawn = jax.random.randint(key, (LAYERS,), TOK_DEV, TOKENS_G + 1, dtype=jnp.int32)
    return drawn.at[0].set(TOKENS_G)


def levels(stream_key, shape, cuts, least, top_value):
    level = 1.0
    for position, blocks in cuts:
        heights = jax.random.uniform(jax.random.fold_in(jax.random.fold_in(stream_key, 6), position), (blocks,), jnp.float32, least / len(cuts), top_value / len(cuts))
        level = level * jnp.repeat(jnp.exp(heights), shape[position] // blocks).reshape((-1,) + (1,) * (len(shape) - 1 - position))
    return level


def assign_block(key, own, number, rows, number_of, top, most, slope):
    ranking = jax.random.permutation(key, number_of)
    heavy_load, common = shares(number_of, rows * top, most, slope, True), shares(number_of, rows * top, most, slope, False)
    places = jnp.arange(number_of)

    def named(sizes, offset_by):
        used = int((sizes > 0).sum())
        fixed = max(1, used // 4)
        moved = fixed + (places - fixed + offset_by * (used - fixed)) % max(1, number_of - fixed)
        return jnp.zeros((number_of,), jnp.int32).at[ranking[jnp.where(places < fixed, places, moved)]].set(jnp.asarray(sizes, jnp.int32))

    sizes = jnp.where(number % 4 == 0, named(heavy_load, number // 4), named(common, number - number // 4 - 1))
    mixed = jax.random.permutation(jax.random.fold_in(own, 3), number_of)
    source_of, receiver = mixed[0:number_of // 2 * 2:2], mixed[1:number_of // 2 * 2:2]
    room = jnp.minimum(sizes[source_of] - 1, most - sizes[receiver]) // 2
    room = jnp.where((source_of == ranking[0]) | (receiver == ranking[0]) | (sizes[receiver] == 0), 0, jnp.maximum(room, 0))
    moved = jax.random.randint(jax.random.fold_in(own, 4), (number_of // 2,), 0, 1 << 20) % (room + 1)
    sizes = sizes.at[source_of].add(-moved).at[receiver].add(moved)
    labels = jnp.searchsorted(jnp.cumsum(sizes), jnp.arange(rows * top), side="right").astype(jnp.int32)
    table = labels.reshape(top, rows).T
    table = table[jax.random.permutation(jax.random.fold_in(own, 1), rows)]
    offset_by = jax.random.randint(jax.random.fold_in(own, 2), (rows, 1), 0, top)
    return jnp.take_along_axis(table, (jnp.arange(top)[None, :] + offset_by) % top, axis=1)


def shares(count, total, bound, slope, full):
    loads = [(1 << 20) // math.isqrt(standing ** slope) + 1 for standing in range(1, count + 1)]
    largest = bound if full else min(bound, max(-(-total // count), total * loads[0] // sum(loads)))
    least = 1 if total - largest >= count - 1 else 0
    given, rest = [largest] + [least] * (count - 1), total - largest - least * (count - 1)
    while rest > 0:
        free = [i for i in range(1, count) if given[i] < largest] or [i for i in range(1, count) if given[i] < bound]
        whole, remaining = sum([loads[i] for i in free]), rest
        for i in free:
            extra = min(bound - given[i], max(1, remaining * loads[i] // whole), rest)
            given[i] = given[i] + extra
            rest = rest - extra
    return np.array(given)


def gaussian(stream_key, shape, width, bound, cuts=(), kind=jnp.bfloat16):
    result = jax.random.normal(stream_key, shape, jnp.float32) * width
    if len(cuts) > 0:
        result = levels(stream_key, shape, cuts, -0.22, 0.18) * result
    return jnp.clip(result, min=-bound, max=bound).astype(kind)


def setup_inputs(seed: int = 0) -> dict:
    splits = jax.random.split(jax.random.key(seed), 9)
    state = gaussian(splits[0], (LAYERS, TOKENS_G, D), 1.0, 6.0, ((0, 16), (1, 16)))
    lengths = draw_lengths(jax.random.fold_in(splits[8], 71), 0)
    gain = jnp.clip(1.0 + 0.15 * jax.random.normal(splits[2], (LAYERS, D), jnp.float32), 0.25, 1.75)
    w_gate = gaussian(splits[3], (LAYERS, D, EXPERTS * FFW), D ** -0.5, 0.09375, ((0, 16), (2, 16)))
    w_up = gaussian(splits[4], (LAYERS, D, EXPERTS * FFW), D ** -0.5, 0.09375, ((0, 16), (2, 16)))
    w_down = gaussian(splits[5], (LAYERS, EXPERTS * FFW, D), FFW ** -0.5, 0.21875, ((0, 16), (1, 16)))
    expert_ids_keys = jax.random.split(jax.random.fold_in(splits[6], 1), STEPS * LAYERS * TOKENS_G // TOK_DEV)
    expert_ids_turns = jax.random.permutation(jax.random.fold_in(splits[6], 3), STEPS * LAYERS * TOKENS_G // TOK_DEV)
    expert_ids = jax.vmap(lambda own, number: assign_block(jax.random.fold_in(splits[6], 2), own, number, TOK_DEV, EXPERTS, TOP, CAP, 2))(expert_ids_keys, expert_ids_turns).reshape((STEPS, LAYERS, TOKENS_G, TOP))
    gate_weights = jnp.clip(jnp.exp(math.log(1.0) - 2.3025851 * jax.random.uniform(splits[7], (STEPS, LAYERS, TOKENS_G, TOP), jnp.float32) ** levels(splits[7], (STEPS, LAYERS, TOKENS_G, TOP), ((1, 16), (2, 16)), -0.2, 0.2)), 0.1, 1.0)
    return {"state": state, "lengths": lengths, "gain": gain, "w_gate": w_gate, "w_up": w_up, "w_down": w_down, "expert_ids": expert_ids, "gate_weights": gate_weights}


def layer(x, gain, w_gate, w_up, w_down, ids, gates, length):
    total_rows = x.shape[0]
    xf = x.astype(jnp.float32)
    normed = (xf * lax.rsqrt(lax.optimization_barrier(jnp.mean(xf * xf, axis=-1, keepdims=True)) + 1e-06) * gain).astype(jnp.bfloat16)
    row_index = jnp.arange(total_rows, dtype=jnp.int32)
    valid = row_index < length
    ids = ids.astype(jnp.int32)
    onehot = ((ids[:, :, None] == jnp.arange(EXPERTS, dtype=jnp.int32)) & valid[:, None, None]).astype(jnp.int32)
    onehot = onehot.reshape(N_EXPERT, TOK_DEV * TOP, EXPERTS)
    before = jnp.cumsum(onehot, axis=1) - onehot
    pos = lax.optimization_barrier(jnp.sum(before * onehot, axis=-1)).reshape(total_rows, TOP).astype(jnp.int32)
    block = jnp.broadcast_to((row_index // TOK_DEV)[:, None], (total_rows, TOP)).astype(jnp.int32)
    pos_live = jnp.where(valid[:, None], pos, CAP).astype(jnp.int32)
    values = jnp.broadcast_to(normed[:, None, :], (total_rows, TOP, D))
    buffer = jnp.zeros((EXPERTS, N_EXPERT, CAP, D), jnp.bfloat16).at[ids, block, pos_live].set(values, mode='drop')
    half = FFW // 2

    def serve(index):
        rows = buffer[index].reshape(N_EXPERT * CAP, D)
        parts = []
        for side in range(2):
            first = (index * FFW + side * half).astype(jnp.int32)
            gate_cols = lax.dynamic_slice_in_dim(w_gate, first, half, 1)
            up_cols = lax.dynamic_slice_in_dim(w_up, first, half, 1)
            down_rows = lax.dynamic_slice_in_dim(w_down, first, half, 0)
            gated = jnp.dot(rows, gate_cols, preferred_element_type=jnp.float32)
            upper = jnp.dot(rows, up_cols, preferred_element_type=jnp.float32)
            hidden = (jax.nn.silu(gated) * upper).astype(jnp.bfloat16)
            parts.append(jnp.dot(hidden, down_rows, preferred_element_type=jnp.float32).astype(jnp.bfloat16))
        merged = (parts[0].astype(jnp.float32) + parts[1].astype(jnp.float32)).astype(jnp.bfloat16)
        return merged.reshape(N_EXPERT, CAP, D)
    outputs = lax.map(serve, jnp.arange(EXPERTS, dtype=jnp.int32))
    fetched = outputs[ids, block, jnp.minimum(pos_live, CAP - 1)]
    weights = jnp.where(valid[:, None], gates, 0.0).astype(jnp.float32)
    total = xf + lax.optimization_barrier(jnp.sum(weights[:, :, None] * fetched.astype(jnp.float32), axis=1))
    return total.astype(jnp.bfloat16)

def reference(state, lengths, gain, w_gate, w_up, w_down, expert_ids, gate_weights):
    lengths = lengths.astype(jnp.int32)
    for step in range(STEPS):

        def apply_section(items):
            return layer(*items)
        moved = lax.map(apply_section, (state, gain, w_gate, w_up, w_down, expert_ids[step], gate_weights[step], lengths))
        state = jnp.roll(moved, 1, axis=0)
        lengths = jnp.roll(lengths, 1, axis=0)
    return state
```

```python
import functools

import jax
import jax.numpy as jnp
from jax import lax
from jax.experimental import pallas as pl
from jax.experimental.pallas import tpu as pltpu
from jax.sharding import PartitionSpec as P

CAP = 40
CHIPS = 8
OWN = 2
CHUNKS = 4
GROUPS = 4
MESH = pl.DeviceIdType.MESH
F32 = jnp.float32
BF16 = jnp.bfloat16


def order(k):
    m = k % 4
    return (2 * m + 1 - m // 2) % 4, (k % 2 + k // 4) % 2


def kernel(
    x_ref, meta_ref, gain_ref, wg_ref, wu_ref, wd_ref, o_ref,
    xin, xb, ssb, meta0, meta1, metaz, gain1, wgu, wdn, normed, pick, pickw, pickt,
    packed, arrived, hidden, outgo, back, stage,
    w_sem, wd_send, wd_recv, x_send, x_recv, ss_send, ss_recv, m_send, m_recv,
    d_send, d_recv, f_send, f_recv, h_send, h_recv, c_send, c_recv, r_send, r_recv, o_send, o_recv, l_sem,
):
    rows = x_ref.shape[0]
    width = x_ref.shape[1]
    half = width // 2
    hid = wg_ref.shape[1]
    block = 2 * CAP
    cw = half // CHUNKS
    per = CHIPS // GROUPS
    section = lax.axis_index("section")
    expert = lax.axis_index("expert")
    depth = lax.axis_size("section") // 2
    z = section // 2
    x_lo = section % 2
    y = expert // 4
    x_hi = (expert // 2) % 2
    core = expert % 2
    other = 1 - core
    chip = expert // 2

    def device(dz=0, flip=0, dy=0, fxh=0, to=None):
        to = core if to is None else to
        return (
            ((z + dz + depth) % depth) * 2 + (x_lo + flip) % 2,
            (((y + dy + 4) % 4) * 2 + (x_hi + fxh) % 2) * 2 + to,
        )

    partner = device(to=other)
    mine = pl.multiple_of(core * half, half)
    theirs = pl.multiple_of(other * half, half)

    def remote(src, dst, send, recv, to):
        return pltpu.make_async_remote_copy(
            src_ref=src, dst_ref=dst, send_sem=send, recv_sem=recv, device_id=to, device_id_type=MESH
        )

    def loop(count, step):
        lax.fori_loop(0, count, lambda i, c: (step(i), c)[1], 0)

    hid_at = pl.multiple_of(core * hid, hid)
    weight_copies = [
        pltpu.make_async_copy(wg_ref, wgu.at[:, pl.ds(0, hid)], w_sem.at[0]),
        pltpu.make_async_copy(wu_ref, wgu.at[:, pl.ds(hid, hid)], w_sem.at[1]),
        pltpu.make_async_copy(wd_ref.at[:, pl.ds(mine, half)], wdn.at[pl.ds(hid_at, hid), :], w_sem.at[2]),
    ]
    own_x = pltpu.make_async_copy(x_ref.at[:, pl.ds(mine, half)], xb.at[0, core], l_sem.at[0])
    whole_x = pltpu.make_async_copy(x_ref, xin, l_sem.at[1])
    own_meta = pltpu.make_async_copy(meta_ref, meta0.at[core], l_sem.at[2])
    whole_x.start()
    own_x.start()
    own_meta.start()

    barrier = pltpu.get_barrier_semaphore()

    def greet(to):
        pl.semaphore_signal(barrier, inc=1, device_id=to, device_id_type=MESH)

    greet(partner)

    def greet_chips(k):
        dy, fxh = order(k)
        greet(device(flip=1, dy=dy, fxh=fxh))

        @pl.when(k != OWN)
        def _():
            greet(device(dy=dy, fxh=fxh))

    loop(CHIPS, greet_chips)
    greet(device(flip=1, to=other))
    for dz in (1, -1):
        for to in (core, other):
            greet(device(dz=dz, to=to))
    pl.semaphore_wait(barrier, 2 * CHIPS + 5)

    x_copy = remote(x_ref.at[:, pl.ds(theirs, half)], xb.at[0, core], x_send, x_recv, partner)
    meta_copies = [
        remote(meta_ref, meta0.at[core], m_send.at[0], m_recv.at[0], partner),
        remote(meta_ref, metaz, m_send.at[1], m_recv.at[1], device(dz=1)),
        remote(gain_ref, gain1, m_send.at[2], m_recv.at[2], device(flip=1)),
        remote(meta_ref, meta1.at[core], m_send.at[3], m_recv.at[3 + core], device(flip=1, to=core)),
        remote(meta_ref, meta1.at[core], m_send.at[4], m_recv.at[3 + core], device(flip=1, to=other)),
    ]
    meta_copies[0].start()
    x_copy.start()
    for copy in weight_copies:
        copy.start()
    whole_x.wait()
    xf = xin[...].astype(F32)
    ssb[0, core] = jnp.broadcast_to(jnp.sum(xf * xf, axis=-1, keepdims=True), (rows, 128))
    ss_copy = remote(ssb.at[0, core], ssb.at[0, core], ss_send.at[0], ss_recv.at[0], partner)
    ss_copy.start()
    for copy in meta_copies[1:]:
        copy.start()
    wd_copy = remote(
        wd_ref.at[:, pl.ds(theirs, half)], wdn.at[pl.ds(hid_at, hid), :], wd_send, wd_recv, partner
    )
    wd_copy.start()
    own_meta.wait()
    own_x.wait()
    meta_copies[0].wait()
    x_copy.wait()
    ss_copy.wait()

    sub8 = lax.broadcasted_iota(jnp.int32, (8, rows), 0).astype(F32)
    before = (
        lax.broadcasted_iota(jnp.int32, (rows, rows), 0) < lax.broadcasted_iota(jnp.int32, (rows, rows), 1)
    ).astype(BF16)
    lane = lax.broadcasted_iota(jnp.int32, (1, rows), 1)
    slot_no = lax.broadcasted_iota(jnp.int32, (block, rows), 0).astype(F32)

    for step in range(2):
        flip = step
        meta = meta1 if step else meta0

        choices = []
        for part in range(2):
            if step == 0:
                length = meta0[part, 8:9, :]
            else:
                length = jnp.where(x_lo == 0, meta0[0, 8:9, :], metaz[8:9, :])
            live = ((chip * 2 + part) * rows + lane).astype(F32) < length
            ids = [meta[part, 2 * step + k : 2 * step + k + 1, :] for k in range(2)]
            gates = [meta[part, 4 + 2 * step + k : 5 + 2 * step + k, :] for k in range(2)]
            ones = [jnp.where((i == sub8) & live, 1.0, 0.0) for i in ids]
            earlier = jnp.dot((ones[0] + ones[1]).astype(BF16), before, preferred_element_type=F32)
            slots = [
                jnp.where(live, jnp.sum(earlier * one, axis=0, keepdims=True) + float(part * CAP), -1.0)
                for one in ones
            ]
            choices.append((ids, gates, slots))

        gain = gain1 if step else gain_ref
        for part in range(2):
            if step == 0:
                total = ssb[0, part, :, 0:1]
            else:
                total = ssb[1, part, :, 0:1] + ssb[2, part, :, 0:1]
            scale = lax.rsqrt(total * (1.0 / width) + 1e-06)
            normed[part * rows : (part + 1) * rows, :] = (
                xb[step, part].astype(F32) * scale * gain[0:1, pl.ds(mine, half)]
            ).astype(BF16)

        def dispatch(k):
            dy, fxh = order(k)
            return remote(
                packed.at[k], arrived.at[step, core, k], d_send.at[k], d_recv.at[step, k],
                device(flip=flip, dy=dy, fxh=fxh),
            )

        def pack(k):
            dy, fxh = order(k)
            target = (((y + dy) % 4) * 2 + (x_hi + fxh) % 2).astype(F32)
            hits, weighted = [], []
            for ids, gates, slots in choices:
                match = [jnp.where((ids[i] == target) & (slots[i] == slot_no), 1.0, 0.0) for i in range(2)]
                hits.append(match[0] + match[1])
                weighted.append(match[0] * gates[0] + match[1] * gates[1])
            pick[...] = jnp.concatenate(hits, axis=1).astype(BF16)
            pickw[k] = jnp.concatenate(weighted, axis=1)
            sent = jnp.dot(pick[...], normed[...], preferred_element_type=F32).astype(BF16)
            if step == 0:

                @pl.when(k == OWN)
                def _():
                    arrived[0, core, OWN] = sent

                @pl.when(k != OWN)
                def _():
                    packed[k] = sent
                    dispatch(k).start()
            else:
                packed[k] = sent
                dispatch(k).start()

        loop(CHIPS, pack)

        turned = pickw[...].reshape(CHIPS * block, 2 * rows).T
        high = turned.astype(BF16)
        pickt[0] = high
        pickt[1] = (turned - high.astype(F32)).astype(BF16)

        if step == 0:
            for copy in weight_copies:
                copy.wait()

        def forward(k):
            return remote(
                arrived.at[step, core, k], arrived.at[step, core, k], f_send.at[k], f_recv.at[step, k], partner
            )

        def forwarded(k):
            return remote(
                arrived.at[step, other, k], arrived.at[step, other, k], f_send.at[k], f_recv.at[step, k], partner
            )

        def share(g):
            place = hidden.at[step, pl.ds(pl.multiple_of(g * per * block, per * block), per * block), pl.ds(hid_at, hid)]
            return remote(place, place, h_send.at[g], h_recv.at[step, g], partner)

        def serve(g):
            for i in range(per):
                k = g * per + i
                if step == 0:

                    @pl.when(k != OWN)
                    def _():
                        dispatch(k).wait_recv()
                else:
                    dispatch(k).wait_recv()
                forward(k).start()
            for i in range(per):
                forwarded(g * per + i).wait_recv()
            both = [
                arrived[step, side, pl.ds(g * per, per)].reshape(per * block, half) for side in range(2)
            ]
            product = jnp.dot(both[0], wgu[0:half, :], preferred_element_type=F32)
            product = product + jnp.dot(both[1], wgu[half:width, :], preferred_element_type=F32)
            value = (jax.nn.silu(product[:, 0:hid]) * product[:, hid:]).astype(BF16)
            hidden[step, pl.ds(pl.multiple_of(g * per * block, per * block), per * block), pl.ds(hid_at, hid)] = value
            share(g).start()

        loop(GROUPS, serve)

        if step == 0:
            wd_copy.wait()
        hid_there = pl.multiple_of(other * hid, hid)

        def shared(g):
            place = hidden.at[step, pl.ds(pl.multiple_of(g * per * block, per * block), per * block), pl.ds(hid_there, hid)]
            return remote(place, place, h_send.at[g], h_recv.at[step, g], partner)

        loop(GROUPS, lambda g: shared(g).wait_recv())

        def give(q, k):
            dy, fxh = order(k)
            return remote(
                outgo.at[q, k], back.at[step, q, k], c_send.at[q, k], c_recv.at[step, q, k],
                device(flip=flip, dy=-dy, fxh=fxh),
            )

        for q in range(CHUNKS):

            def finish(g):
                at = pl.multiple_of(g * per * block, per * block)
                value = jnp.dot(
                    hidden[step, pl.ds(at, per * block), :], wdn[:, q * cw : (q + 1) * cw],
                    preferred_element_type=F32,
                ).astype(BF16).reshape(per, block, cw)
                for i in range(per):
                    k = g * per + i
                    if step == 0:

                        @pl.when(k == OWN)
                        def _():
                            back[0, q, OWN] = value[i]

                        @pl.when(k != OWN)
                        def _():
                            outgo[q, k] = value[i]
                            give(q, k).start()
                    else:
                        outgo[q, k] = value[i]
                        give(q, k).start()

            loop(GROUPS, finish)

        def relay(q):
            return remote(
                stage.at[0, q], xb.at[1, :, :, pl.ds(q * cw, cw)], r_send.at[q], r_recv.at[q], device(dz=1)
            )

        def hand(q, part, dz):
            columns = pl.ds(pl.multiple_of(core * half + q * cw, cw), cw)
            return remote(
                stage.at[1, q, part], o_ref.at[:, columns], o_send.at[q, part], o_recv.at[q, core],
                device(dz=dz, to=part),
            )

        def keep(q):
            columns = pl.ds(pl.multiple_of(core * half + q * cw, cw), cw)
            return pltpu.make_async_copy(stage.at[1, q, core], o_ref.at[:, columns], l_sem.at[3 + q])

        for q in range(CHUNKS):

            def landed(k):
                if step == 0:

                    @pl.when(k != OWN)
                    def _():
                        give(q, k).wait_recv()
                else:
                    give(q, k).wait_recv()

            loop(CHIPS, landed)
            results = back[step, q].reshape(CHIPS * block, cw)
            for part in range(2):
                value = jnp.dot(pickt[0, part * rows : (part + 1) * rows, :], results, preferred_element_type=F32)
                value = value + jnp.dot(
                    pickt[1, part * rows : (part + 1) * rows, :], results, preferred_element_type=F32
                )
                value = (xb[step, part, :, q * cw : (q + 1) * cw].astype(F32) + value).astype(BF16)
                stage[step, q, part] = value

            if step == 0:

                @pl.when(x_lo == 1)
                def _():
                    relay(q).start()

                @pl.when(x_lo == 0)
                def _():
                    xb[1, :, :, q * cw : (q + 1) * cw] = stage[0, q]
            else:

                @pl.when(x_lo == 0)
                def _():
                    for part in range(2):
                        hand(q, part, 1).start()

                @pl.when(x_lo == 1)
                def _():
                    hand(q, other, 0).start()
                    keep(q).start()

        def sent_all(k):
            forward(k).wait_send()
            if step == 0:

                @pl.when(k != OWN)
                def _():
                    dispatch(k).wait_send()
                    for q in range(CHUNKS):
                        give(q, k).wait_send()
            else:
                dispatch(k).wait_send()
                for q in range(CHUNKS):
                    give(q, k).wait_send()

        if step == 0:
            for copy in meta_copies[1:3]:
                copy.wait()
            for copy in meta_copies[3:]:
                copy.wait_send()
            for part in range(2):
                remote(
                    meta_ref, meta1.at[part], m_send.at[3], m_recv.at[3 + part], device(flip=1, to=part)
                ).wait_recv()

            @pl.when(x_lo == 1)
            def _():
                for q in range(CHUNKS):
                    relay(q).wait()

            for part in range(2):
                value = xb[1, part].astype(F32)
                ssb[1, part] = jnp.broadcast_to(jnp.sum(value * value, axis=-1, keepdims=True), (rows, 128))
            sums = remote(ssb.at[1], ssb.at[2], ss_send.at[1], ss_recv.at[1], partner)
            sums.start()
            loop(CHIPS, sent_all)
            loop(GROUPS, lambda g: share(g).wait_send())
            sums.wait()
        else:
            loop(CHIPS, sent_all)
            loop(GROUPS, lambda g: share(g).wait_send())

            @pl.when(x_lo == 0)
            def _():
                for q in range(CHUNKS):
                    for part in range(2):
                        hand(q, part, 1).wait_send()

            @pl.when(x_lo == 1)
            def _():
                for q in range(CHUNKS):
                    hand(q, other, 0).wait_send()
                    keep(q).wait()

            def taken(q, part):
                columns = pl.ds(part * half + q * cw, cw)
                remote(
                    stage.at[1, q, 0], o_ref.at[:, columns], o_send.at[q, 0], o_recv.at[q, part], partner
                ).wait_recv()

            @pl.when(x_lo == 0)
            def _():
                for q in range(CHUNKS):
                    for part in range(2):
                        taken(q, part)

            @pl.when((x_lo == 1) & (core == 0))
            def _():
                for q in range(CHUNKS):
                    taken(q, 1)

            @pl.when((x_lo == 1) & (core == 1))
            def _():
                for q in range(CHUNKS):
                    taken(q, 0)


def body(state, lengths, gain, w_gate, w_up, w_down, expert_ids, gate_weights):
    rows, width = state.shape[1:]
    hid = w_gate.shape[2]
    half = width // 2
    block = 2 * CAP
    cw = half // CHUNKS
    meta = jnp.concatenate(
        [
            expert_ids[:, 0].transpose(0, 2, 1).reshape(4, rows).astype(F32),
            gate_weights[:, 0].transpose(0, 2, 1).reshape(4, rows),
            jnp.broadcast_to(lengths.astype(F32)[:, None], (8, rows)),
        ],
        axis=0,
    )
    vmem = pl.BlockSpec(memory_space=pltpu.VMEM)
    anywhere = pl.BlockSpec(memory_space=pl.ANY)
    dma = pltpu.SemaphoreType.DMA
    out = pl.pallas_call(
        kernel,
        out_shape=jax.ShapeDtypeStruct((rows, width), BF16),
        in_specs=[anywhere, vmem, vmem, anywhere, anywhere, anywhere],
        out_specs=anywhere,
        scratch_shapes=[
            pltpu.VMEM((rows, width), BF16),
            pltpu.VMEM((2, 2, rows, half), BF16),
            pltpu.VMEM((3, 2, rows, 128), F32),
            pltpu.VMEM((2, 16, rows), F32),
            pltpu.VMEM((2, 16, rows), F32),
            pltpu.VMEM((16, rows), F32),
            pltpu.VMEM((1, width), F32),
            pltpu.VMEM((width, 2 * hid), BF16),
            pltpu.VMEM((2 * hid, half), BF16),
            pltpu.VMEM((2 * rows, half), BF16),
            pltpu.VMEM((block, 2 * rows), BF16),
            pltpu.VMEM((CHIPS, block, 2 * rows), F32),
            pltpu.VMEM((2, 2 * rows, CHIPS * block), BF16),
            pltpu.VMEM((CHIPS, block, half), BF16),
            pltpu.VMEM((2, 2, CHIPS, block, half), BF16),
            pltpu.VMEM((2, CHIPS * block, 2 * hid), BF16),
            pltpu.VMEM((CHUNKS, CHIPS, block, cw), BF16),
            pltpu.VMEM((2, CHUNKS, CHIPS, block, cw), BF16),
            pltpu.VMEM((2, CHUNKS, 2, rows, cw), BF16),
            dma((3,)),
            dma, dma,
            dma, dma,
            dma((2,)), dma((2,)),
            dma((5,)), dma((5,)),
            dma((CHIPS,)), dma((2, CHIPS)),
            dma((CHIPS,)), dma((2, CHIPS)),
            dma((GROUPS,)), dma((2, GROUPS)),
            dma((CHUNKS, CHIPS)), dma((2, CHUNKS, CHIPS)),
            dma((CHUNKS,)), dma((CHUNKS,)),
            dma((CHUNKS, 2)), dma((CHUNKS, 2)),
            dma((3 + CHUNKS,)),
        ],
        compiler_params=pltpu.CompilerParams(
            collective_id=0, has_side_effects=True, vmem_limit_bytes=58 * 2**20
        ),
        cost_estimate=pl.CostEstimate(
            flops=2 * 2 * CHIPS * block * width * 3 * hid, bytes_accessed=3 * width * hid * 2 + 2 * rows * width * 2,
            transcendentals=0,
        ),
    )(state[0], meta, gain, w_gate[0], w_up[0], w_down[0])
    return out[None]


def solution(mesh):
    return jax.shard_map(
        body,
        mesh=mesh,
        in_specs=(
            P("section", "expert", None),
            P("section"),
            P("section", None),
            P("section", None, "expert"),
            P("section", None, "expert"),
            P("section", "expert", None),
            P(None, "section", "expert", None),
            P(None, "section", "expert", None),
        ),
        out_specs=P("section", "expert", None),
        check_vma=False,
    )
```

```python
import functools

import jax
import jax.numpy as jnp
from jax import lax
from jax.experimental import pallas as pl
from jax.experimental.pallas import tpu as pltpu
from jax.sharding import PartitionSpec as P

CAP = 40
CHIPS = 8
OWN = 2
CHUNKS = 8
GROUPS = 4
EARLY = 2
MESH = pl.DeviceIdType.MESH
F32 = jnp.float32
BF16 = jnp.bfloat16


def order(k):
    m = k % 4
    return (2 * m + 1 - m // 2) % 4, (k % 2 + k // 4) % 2


def kernel(
    x_ref, meta_ref, gain_ref, wg_ref, wu_ref, wd_ref, o_ref,
    xin, xb, ssb, ssl, meta0, meta1, metaz, gain1, wgu, wdn, normed, pick, pickw, pickt,
    packed, arrived, hidden, outgo, back, stage,
    w_sem, wd_send, wd_recv, x_send, x_recv, ss_send, ss_recv, m_send, m_recv,
    d_send, d_recv, f_send, f_recv, h_send, h_recv, c_send, c_recv, r_send, r_recv, o_send, o_recv, l_sem,
):
    rows = x_ref.shape[0]
    width = x_ref.shape[1]
    half = width // 2
    hid = wg_ref.shape[1]
    block = 2 * CAP
    cw = half // CHUNKS
    per = CHIPS // GROUPS
    section = lax.axis_index("section")
    expert = lax.axis_index("expert")
    depth = lax.axis_size("section") // 2
    z = section // 2
    x_lo = section % 2
    y = expert // 4
    x_hi = (expert // 2) % 2
    core = expert % 2
    other = 1 - core
    chip = expert // 2

    def device(dz=0, flip=0, dy=0, fxh=0, to=None):
        to = core if to is None else to
        return (
            ((z + dz + depth) % depth) * 2 + (x_lo + flip) % 2,
            (((y + dy + 4) % 4) * 2 + (x_hi + fxh) % 2) * 2 + to,
        )

    partner = device(to=other)
    mine = pl.multiple_of(core * half, half)
    theirs = pl.multiple_of(other * half, half)

    def remote(src, dst, send, recv, to):
        return pltpu.make_async_remote_copy(
            src_ref=src, dst_ref=dst, send_sem=send, recv_sem=recv, device_id=to, device_id_type=MESH
        )

    def loop(first, last, step):
        lax.fori_loop(first, last, lambda i, c: (step(i), c)[1], 0)

    hid_at = pl.multiple_of(core * hid, hid)
    hid_there = pl.multiple_of(other * hid, hid)
    weight_copies = [
        pltpu.make_async_copy(wg_ref, wgu.at[:, pl.ds(0, hid)], w_sem.at[0]),
        pltpu.make_async_copy(wu_ref, wgu.at[:, pl.ds(hid, hid)], w_sem.at[1]),
        pltpu.make_async_copy(wd_ref.at[:, pl.ds(mine, half)], wdn.at[pl.ds(hid_at, hid), :], w_sem.at[2]),
    ]
    own_x = pltpu.make_async_copy(x_ref.at[:, pl.ds(mine, half)], xb.at[0, core], l_sem.at[0])
    whole_x = pltpu.make_async_copy(x_ref, xin, l_sem.at[1])
    own_meta = pltpu.make_async_copy(meta_ref, meta0.at[core], l_sem.at[2])
    whole_x.start()
    own_x.start()
    own_meta.start()

    barrier = pltpu.get_barrier_semaphore()

    def greet(to):
        pl.semaphore_signal(barrier, inc=1, device_id=to, device_id_type=MESH)

    greet(partner)

    def greet_chips(k):
        dy, fxh = order(k)
        greet(device(flip=1, dy=dy, fxh=fxh))

        @pl.when(k != OWN)
        def _():
            greet(device(dy=dy, fxh=fxh))

    loop(0, CHIPS, greet_chips)
    greet(device(flip=1, to=other))
    for dz in (1, -1):
        for to in (core, other):
            greet(device(dz=dz, to=to))
    for copy in weight_copies:
        copy.start()
    whole_x.wait()
    xf = xin[...].astype(F32)
    ssb[0, core] = jnp.broadcast_to(jnp.sum(xf * xf, axis=-1, keepdims=True), (rows, 128))
    pl.semaphore_wait(barrier, 2 * CHIPS + 5)

    x_copy = remote(x_ref.at[:, pl.ds(theirs, half)], xb.at[0, core], x_send, x_recv, partner)
    meta_copies = [
        remote(meta_ref, meta0.at[core], m_send.at[0], m_recv.at[0], partner),
        remote(meta_ref, metaz, m_send.at[1], m_recv.at[1], device(dz=1)),
        remote(gain_ref, gain1, m_send.at[2], m_recv.at[2], device(flip=1)),
        remote(meta_ref, meta1.at[core], m_send.at[3], m_recv.at[3 + core], device(flip=1, to=core)),
        remote(meta_ref, meta1.at[core], m_send.at[4], m_recv.at[3 + core], device(flip=1, to=other)),
    ]
    ss_copy = remote(ssb.at[0, core], ssb.at[0, core], ss_send.at[0], ss_recv.at[0], partner)
    meta_copies[0].start()
    x_copy.start()
    ss_copy.start()
    for copy in meta_copies[1:]:
        copy.start()
    wd_copy = remote(
        wd_ref.at[:, pl.ds(theirs, half)], wdn.at[pl.ds(hid_at, hid), :], wd_send, wd_recv, partner
    )
    wd_copy.start()

    sub8 = lax.broadcasted_iota(jnp.int32, (8, rows), 0).astype(F32)
    before = (
        lax.broadcasted_iota(jnp.int32, (rows, rows), 0) < lax.broadcasted_iota(jnp.int32, (rows, rows), 1)
    ).astype(BF16)
    lane = lax.broadcasted_iota(jnp.int32, (1, rows), 1)
    slot_no = lax.broadcasted_iota(jnp.int32, (block, rows), 0).astype(F32)

    def choose(step):
        meta = meta1 if step else meta0
        choices = []
        for part in range(2):
            if step == 0:
                length = meta0[part, 8:9, :]
            else:
                length = jnp.where(x_lo == 0, meta0[0, 8:9, :], metaz[8:9, :])
            live = ((chip * 2 + part) * rows + lane).astype(F32) < length
            ids = [meta[part, 2 * step + k : 2 * step + k + 1, :] for k in range(2)]
            gates = [meta[part, 4 + 2 * step + k : 5 + 2 * step + k, :] for k in range(2)]
            ones = [jnp.where((i == sub8) & live, 1.0, 0.0) for i in ids]
            earlier = jnp.dot((ones[0] + ones[1]).astype(BF16), before, preferred_element_type=F32)
            slots = [
                jnp.where(live, jnp.sum(earlier * one, axis=0, keepdims=True) + float(part * CAP), -1.0)
                for one in ones
            ]
            choices.append((ids, gates, slots))

        def match_chip(k):
            dy, fxh = order(k)
            target = (((y + dy) % 4) * 2 + (x_hi + fxh) % 2).astype(F32)
            hits, weighted = [], []
            for ids, gates, slots in choices:
                match = [jnp.where((ids[i] == target) & (slots[i] == slot_no), 1.0, 0.0) for i in range(2)]
                hits.append(match[0] + match[1])
                weighted.append(match[0] * gates[0] + match[1] * gates[1])
            pick[k] = jnp.concatenate(hits, axis=1).astype(BF16)
            pickw[k] = jnp.concatenate(weighted, axis=1)

        loop(0, CHIPS, match_chip)

    def turn(step):
        turned = pickw[...].reshape(CHIPS * block, 2 * rows).T
        high = turned.astype(BF16)
        pickt[step, 0 : 2 * rows] = high
        pickt[step, 2 * rows :] = (turned - high.astype(F32)).astype(BF16)

    def norm(step, part, total):
        gain = gain1 if step else gain_ref
        scale = lax.rsqrt(total * (1.0 / width) + 1e-06)
        normed[pl.ds(pl.multiple_of(part * rows, rows), rows), :] = (
            xb[step, part].astype(F32) * scale * gain[0:1, pl.ds(mine, half)]
        ).astype(BF16)

    own_meta.wait()
    meta_copies[0].wait()
    choose(0)

    for step in range(2):
        flip = step

        if step == 0:
            own_x.wait()
            norm(0, core, ssb[0, core, :, 0:1])
            x_copy.wait()
            ss_copy.wait()
            norm(0, other, ssb[0, other, :, 0:1])
        else:
            for part in range(2):
                norm(1, part, jnp.sum(ssb[1, part] + ssb[2, part], axis=-1, keepdims=True))

        def dispatch(k):
            dy, fxh = order(k)
            return remote(
                packed.at[k], arrived.at[step, core, k], d_send.at[k], d_recv.at[step, k],
                device(flip=flip, dy=dy, fxh=fxh),
            )

        for pair in range(CHIPS // 2):
            sent = jnp.dot(
                pick[2 * pair : 2 * pair + 2].reshape(2 * block, 2 * rows), normed[...], preferred_element_type=F32
            ).astype(BF16).reshape(2, block, half)
            for i in range(2):
                k = 2 * pair + i
                if step == 0 and k == OWN:
                    arrived[0, core, OWN] = sent[i]
                else:
                    packed[k] = sent[i]
                    dispatch(k).start()

        if step == 0:
            turn(0)
            for copy in weight_copies:
                copy.wait()
            wd_copy.wait()

        def forward(k, side):
            place = arrived.at[step, side, k]
            return remote(place, place, f_send.at[k], f_recv.at[step, k], partner)

        def share(g, at):
            place = hidden.at[
                step, pl.ds(pl.multiple_of(g * per * block, per * block), per * block), pl.ds(at, hid)
            ]
            return remote(place, place, h_send.at[g], h_recv.at[step, g], partner)

        def serve(g):
            for i in range(per):
                k = g * per + i
                if step == 0:

                    @pl.when(k != OWN)
                    def _():
                        dispatch(k).wait_recv()
                else:
                    dispatch(k).wait_recv()
                forward(k, core).start()
            for i in range(per):
                forward(g * per + i, other).wait_recv()
            both = [
                arrived[step, side, pl.ds(g * per, per)].reshape(per * block, half) for side in range(2)
            ]
            product = jnp.dot(both[0], wgu[0:half, :], preferred_element_type=F32)
            product = product + jnp.dot(both[1], wgu[half:width, :], preferred_element_type=F32)
            value = (jax.nn.silu(product[:, 0:hid]) * product[:, hid:]).astype(BF16)
            hidden[step, pl.ds(pl.multiple_of(g * per * block, per * block), per * block), pl.ds(hid_at, hid)] = value
            share(g, hid_at).start()

        def give(q, k):
            dy, fxh = order(k)
            return remote(
                outgo.at[q, k], back.at[step, q, k], c_send.at[q, k], c_recv.at[step, q, k],
                device(flip=flip, dy=-dy, fxh=fxh),
            )

        def finish(q, first, count):
            value = jnp.dot(
                hidden[step, first * per * block : (first + count) * per * block, :],
                wdn[:, pl.ds(pl.multiple_of(q * cw, cw), cw)],
                preferred_element_type=F32,
            ).astype(BF16).reshape(count * per, block, cw)
            for i in range(count * per):
                k = first * per + i
                if step == 0 and k == OWN:
                    back[0, q, OWN] = value[i]
                else:
                    outgo[q, k] = value[i]
                    give(q, k).start()

        loop(0, GROUPS - 1, serve)
        loop(0, GROUPS - 1, lambda g: share(g, hid_there).wait_recv())
        loop(0, EARLY, lambda q: finish(q, 0, GROUPS - 1))
        serve(GROUPS - 1)
        share(GROUPS - 1, hid_there).wait_recv()
        loop(0, EARLY, lambda q: finish(q, GROUPS - 1, 1))
        loop(EARLY, CHUNKS, lambda q: finish(q, 0, GROUPS))

        if step == 0:
            for copy in meta_copies[1:3]:
                copy.wait()
            for copy in meta_copies[3:]:
                copy.wait_send()
            for part in range(2):
                remote(
                    meta_ref, meta1.at[part], m_send.at[3], m_recv.at[3 + part], device(flip=1, to=part)
                ).wait_recv()
            choose(1)
            turn(1)

        def relay(q):
            return remote(
                stage.at[0, q], xb.at[1, :, :, pl.ds(pl.multiple_of(q * cw, cw), cw)],
                r_send.at[q], r_recv.at[q], device(dz=1),
            )

        def hand(q, part, dz):
            columns = pl.ds(pl.multiple_of(core * half + q * cw, cw), cw)
            return remote(
                stage.at[1, q, part], o_ref.at[:, columns], o_send.at[q, part], o_recv.at[q, core],
                device(dz=dz, to=part),
            )

        def keep(q):
            columns = pl.ds(pl.multiple_of(core * half + q * cw, cw), cw)
            return pltpu.make_async_copy(stage.at[1, q, core], o_ref.at[:, columns], l_sem.at[3 + q])

        def combine(q):
            for k in range(CHIPS):
                if not (step == 0 and k == OWN):
                    give(q, k).wait_recv()
            at = pl.multiple_of(q * cw, cw)
            value = jnp.dot(
                pickt[step], back[step, q].reshape(CHIPS * block, cw), preferred_element_type=F32
            )
            for part in range(2):
                low = (2 + part) * rows
                new = (
                    xb[step, part, :, pl.ds(at, cw)].astype(F32)
                    + (value[part * rows : (part + 1) * rows] + value[low : low + rows])
                ).astype(BF16)
                stage[step, q, part] = new
                if step == 0:
                    square = new.astype(F32) * new.astype(F32)
                    sums = square[:, 0:128]
                    for i in range(1, cw // 128):
                        sums = sums + square[:, i * 128 : (i + 1) * 128]
                    ssl[part] += sums

            if step == 0:

                @pl.when(x_lo == 1)
                def _():
                    relay(q).start()

                @pl.when(x_lo == 0)
                def _():
                    xb[1, :, :, pl.ds(at, cw)] = stage[0, q]
            else:

                @pl.when(x_lo == 0)
                def _():
                    for part in range(2):
                        hand(q, part, 1).start()

                @pl.when(x_lo == 1)
                def _():
                    hand(q, other, 0).start()
                    keep(q).start()

        if step == 0:
            ssl[...] = jnp.zeros_like(ssl)
        loop(0, CHUNKS, combine)

        def sent_all(k):
            forward(k, core).wait_send()
            if step == 0:

                @pl.when(k != OWN)
                def _():
                    dispatch(k).wait_send()
                    loop(0, CHUNKS, lambda q: give(q, k).wait_send())
            else:
                dispatch(k).wait_send()
                loop(0, CHUNKS, lambda q: give(q, k).wait_send())

        def all_sent():
            loop(0, CHIPS, sent_all)
            loop(0, GROUPS, lambda g: share(g, hid_at).wait_send())

        if step == 0:
            def sums(to, dz, number, sender):
                return remote(ssl, ssb.at[1 + sender], ss_send.at[number], ss_recv.at[1 + sender], device(dz=dz, to=to))

            @pl.when(x_lo == 0)
            def _():
                sums(other, 0, 1, core).start()
                ssb[1 + core] = ssl[...]
                all_sent()
                sums(other, 0, 1, core).wait_send()
                sums(other, 0, 1, other).wait_recv()

            @pl.when(x_lo == 1)
            def _():
                sums(core, 1, 1, core).start()
                sums(other, 1, 2, core).start()
                all_sent()
                loop(0, CHUNKS, lambda q: relay(q).wait())
                for number, sender in ((1, core), (2, other)):
                    sums(sender, 1, number, core).wait_send()
                    sums(sender, 1, number, sender).wait_recv()
        else:
            all_sent()

            @pl.when(x_lo == 0)
            def _():
                for part in range(2):
                    loop(0, CHUNKS, lambda q: hand(q, part, 1).wait_send())

            @pl.when(x_lo == 1)
            def _():
                loop(0, CHUNKS, lambda q: hand(q, other, 0).wait_send())
                loop(0, CHUNKS, lambda q: keep(q).wait())

            def taken(q, part):
                columns = pl.ds(pl.multiple_of(part * half + q * cw, cw), cw)
                remote(
                    stage.at[1, q, 0], o_ref.at[:, columns], o_send.at[q, 0], o_recv.at[q, part], partner
                ).wait_recv()

            @pl.when(x_lo == 0)
            def _():
                for part in range(2):
                    loop(0, CHUNKS, lambda q: taken(q, part))

            @pl.when(x_lo == 1)
            def _():
                loop(0, CHUNKS, lambda q: taken(q, other))


def body(state, lengths, gain, w_gate, w_up, w_down, expert_ids, gate_weights):
    rows, width = state.shape[1:]
    hid = w_gate.shape[2]
    half = width // 2
    block = 2 * CAP
    cw = half // CHUNKS
    meta = jnp.concatenate(
        [
            expert_ids[:, 0].transpose(0, 2, 1).reshape(4, rows).astype(F32),
            gate_weights[:, 0].transpose(0, 2, 1).reshape(4, rows),
            jnp.broadcast_to(lengths.astype(F32)[:, None], (8, rows)),
        ],
        axis=0,
    )
    vmem = pl.BlockSpec(memory_space=pltpu.VMEM)
    anywhere = pl.BlockSpec(memory_space=pl.ANY)
    dma = pltpu.SemaphoreType.DMA
    out = pl.pallas_call(
        kernel,
        out_shape=jax.ShapeDtypeStruct((rows, width), BF16),
        in_specs=[anywhere, vmem, vmem, anywhere, anywhere, anywhere],
        out_specs=anywhere,
        scratch_shapes=[
            pltpu.VMEM((rows, width), BF16),
            pltpu.VMEM((2, 2, rows, half), BF16),
            pltpu.VMEM((3, 2, rows, 128), F32),
            pltpu.VMEM((2, rows, 128), F32),
            pltpu.VMEM((2, 16, rows), F32),
            pltpu.VMEM((2, 16, rows), F32),
            pltpu.VMEM((16, rows), F32),
            pltpu.VMEM((1, width), F32),
            pltpu.VMEM((width, 2 * hid), BF16),
            pltpu.VMEM((2 * hid, half), BF16),
            pltpu.VMEM((2 * rows, half), BF16),
            pltpu.VMEM((CHIPS, block, 2 * rows), BF16),
            pltpu.VMEM((CHIPS, block, 2 * rows), F32),
            pltpu.VMEM((2, 4 * rows, CHIPS * block), BF16),
            pltpu.VMEM((CHIPS, block, half), BF16),
            pltpu.VMEM((2, 2, CHIPS, block, half), BF16),
            pltpu.VMEM((2, CHIPS * block, 2 * hid), BF16),
            pltpu.VMEM((CHUNKS, CHIPS, block, cw), BF16),
            pltpu.VMEM((2, CHUNKS, CHIPS, block, cw), BF16),
            pltpu.VMEM((2, CHUNKS, 2, rows, cw), BF16),
            dma((3,)),
            dma, dma,
            dma, dma,
            dma((3,)), dma((3,)),
            dma((5,)), dma((5,)),
            dma((CHIPS,)), dma((2, CHIPS)),
            dma((CHIPS,)), dma((2, CHIPS)),
            dma((GROUPS,)), dma((2, GROUPS)),
            dma((CHUNKS, CHIPS)), dma((2, CHUNKS, CHIPS)),
            dma((CHUNKS,)), dma((CHUNKS,)),
            dma((CHUNKS, 2)), dma((CHUNKS, 2)),
            dma((3 + CHUNKS,)),
        ],
        compiler_params=pltpu.CompilerParams(
            collective_id=0, has_side_effects=True, vmem_limit_bytes=58 * 2**20
        ),
        cost_estimate=pl.CostEstimate(
            flops=2 * 2 * CHIPS * block * width * 3 * hid, bytes_accessed=3 * width * hid * 2 + 2 * rows * width * 2,
            transcendentals=0,
        ),
    )(state[0], meta, gain, w_gate[0], w_up[0], w_down[0])
    return out[None]


def solution(mesh):
    return jax.shard_map(
        body,
        mesh=mesh,
        in_specs=(
            P("section", "expert", None),
            P("section"),
            P("section", None),
            P("section", None, "expert"),
            P("section", None, "expert"),
            P("section", "expert", None),
            P(None, "section", "expert", None),
            P(None, "section", "expert", None),
        ),
        out_specs=P("section", "expert", None),
        check_vma=False,
    )
```

```python
import functools

import jax
import jax.numpy as jnp
from jax import lax
from jax.experimental import pallas as pl
from jax.experimental.pallas import tpu as pltpu
from jax.sharding import PartitionSpec as P

CAP = 40
CHIPS = 8
OWN = 2
CHUNKS = 8
GROUPS = 4
STREAM = 4
LAG = 1
EARLY = 2
MESH = pl.DeviceIdType.MESH
F32 = jnp.float32
BF16 = jnp.bfloat16


def order(k):
    m = k % 4
    return (2 * m + 1 - m // 2) % 4, (k % 2 + k // 4) % 2


def kernel(
    x_ref, meta_ref, gain_ref, wg_ref, wu_ref, wd_ref, o_ref,
    xb, meta0, meta1, metaz, gain_t, wgu, wdn, pick, pickw, pickt,
    packed, arrived, hidden, outgo, back, stage,
    w_sem, wd_send, wd_recv, x_send, x_recv, m_send, m_recv,
    d_send, d_recv, f_send, f_recv, h_send, h_recv, c_send, c_recv, r_send, r_recv, o_send, o_recv, l_sem,
):
    rows = x_ref.shape[0]
    width = x_ref.shape[1]
    half = width // 2
    hid = wg_ref.shape[1]
    block = 2 * CAP
    cw = half // CHUNKS
    per = CHIPS // GROUPS
    section = lax.axis_index("section")
    expert = lax.axis_index("expert")
    depth = lax.axis_size("section") // 2
    z = section // 2
    x_lo = section % 2
    y = expert // 4
    x_hi = (expert // 2) % 2
    core = expert % 2
    other = 1 - core
    chip = expert // 2

    def device(dz=0, flip=0, dy=0, fxh=0, to=None):
        to = core if to is None else to
        return (
            ((z + dz + depth) % depth) * 2 + (x_lo + flip) % 2,
            (((y + dy + 4) % 4) * 2 + (x_hi + fxh) % 2) * 2 + to,
        )

    partner = device(to=other)
    mine = pl.multiple_of(core * half, half)
    theirs = pl.multiple_of(other * half, half)

    def remote(src, dst, send, recv, to):
        return pltpu.make_async_remote_copy(
            src_ref=src, dst_ref=dst, send_sem=send, recv_sem=recv, device_id=to, device_id_type=MESH
        )

    def loop(first, last, step):
        lax.fori_loop(first, last, lambda i, c: (step(i), c)[1], 0)

    hid_at = pl.multiple_of(core * hid, hid)
    hid_there = pl.multiple_of(other * hid, hid)
    weight_copies = [
        pltpu.make_async_copy(wg_ref, wgu.at[:, pl.ds(0, hid)], w_sem.at[0]),
        pltpu.make_async_copy(wu_ref, wgu.at[:, pl.ds(hid, hid)], w_sem.at[1]),
        pltpu.make_async_copy(wd_ref.at[:, pl.ds(mine, half)], wdn.at[pl.ds(hid_at, hid), :], w_sem.at[2]),
    ]
    own_x = pltpu.make_async_copy(x_ref.at[:, pl.ds(mine, half)], xb.at[0, core], l_sem.at[0])
    own_meta = pltpu.make_async_copy(meta_ref, meta0.at[core], l_sem.at[2])
    own_x.start()
    own_meta.start()

    barrier = pltpu.get_barrier_semaphore()

    def greet(to):
        pl.semaphore_signal(barrier, inc=1, device_id=to, device_id_type=MESH)

    greet(partner)

    def greet_chips(k):
        dy, fxh = order(k)
        greet(device(flip=1, dy=dy, fxh=fxh))

        @pl.when(k != OWN)
        def _():
            greet(device(dy=dy, fxh=fxh))

    loop(0, CHIPS, greet_chips)
    greet(device(flip=1, to=other))
    for dz in (1, -1):
        for to in (core, other):
            greet(device(dz=dz, to=to))
    for copy in weight_copies:
        copy.start()
    pl.semaphore_wait(barrier, 2 * CHIPS + 5)

    x_copy = remote(x_ref.at[:, pl.ds(theirs, half)], xb.at[0, core], x_send, x_recv, partner)
    meta_copies = [
        remote(meta_ref, meta0.at[core], m_send.at[0], m_recv.at[0], partner),
        remote(meta_ref, metaz, m_send.at[1], m_recv.at[1], device(dz=1)),
        remote(meta_ref, meta1.at[core], m_send.at[2], m_recv.at[2 + core], device(flip=1, to=core)),
        remote(meta_ref, meta1.at[core], m_send.at[3], m_recv.at[2 + core], device(flip=1, to=other)),
    ]
    meta_copies[0].start()
    x_copy.start()
    for copy in meta_copies[1:]:
        copy.start()
    wd_copy = remote(
        wd_ref.at[:, pl.ds(theirs, half)], wdn.at[pl.ds(hid_at, hid), :], wd_send, wd_recv, partner
    )
    wd_copy.start()

    sub8 = lax.broadcasted_iota(jnp.int32, (8, rows), 0).astype(F32)
    before = (
        lax.broadcasted_iota(jnp.int32, (rows, rows), 0) < lax.broadcasted_iota(jnp.int32, (rows, rows), 1)
    ).astype(BF16)
    lane = lax.broadcasted_iota(jnp.int32, (1, rows), 1)
    slot_no = lax.broadcasted_iota(jnp.int32, (block, rows), 0).astype(F32)

    def choose(step):
        meta = meta1 if step else meta0
        choices = []
        for part in range(2):
            if step == 0:
                length = meta0[part, 8:9, :]
            else:
                length = jnp.where(x_lo == 0, meta0[0, 8:9, :], metaz[8:9, :])
            live = ((chip * 2 + part) * rows + lane).astype(F32) < length
            ids = [meta[part, 2 * step + k : 2 * step + k + 1, :] for k in range(2)]
            gates = [meta[part, 4 + 2 * step + k : 5 + 2 * step + k, :] for k in range(2)]
            ones = [jnp.where((i == sub8) & live, 1.0, 0.0) for i in ids]
            earlier = jnp.dot((ones[0] + ones[1]).astype(BF16), before, preferred_element_type=F32)
            slots = [
                jnp.where(live, jnp.sum(earlier * one, axis=0, keepdims=True) + float(part * CAP), -1.0)
                for one in ones
            ]
            choices.append((ids, gates, slots))

        def match_chip(k):
            dy, fxh = order(k)
            target = (((y + dy) % 4) * 2 + (x_hi + fxh) % 2).astype(F32)
            hits, weighted = [], []
            for ids, gates, slots in choices:
                match = [jnp.where((ids[i] == target) & (slots[i] == slot_no), 1.0, 0.0) for i in range(2)]
                hits.append(match[0] + match[1])
                weighted.append(match[0] * gates[0] + match[1] * gates[1])
            pick[k] = jnp.concatenate(hits, axis=1).astype(BF16)
            pickw[k] = jnp.concatenate(weighted, axis=1)

        loop(0, CHIPS, match_chip)

    def turn(step):
        turned = pickw[...].reshape(CHIPS * block, 2 * rows).T
        high = turned.astype(BF16)
        pickt[step, 0 : 2 * rows] = high
        pickt[step, 2 * rows :] = (turned - high.astype(F32)).astype(BF16)

    def scale_weights(j):
        at = pl.multiple_of(j * 128, 128)
        column = jnp.sum(
            jnp.where(lax.broadcasted_iota(jnp.int32, (128, 128), 1) == j, gain_t[...], 0.0), axis=1, keepdims=True
        )
        wgu[pl.ds(at, 128), :] = (wgu[pl.ds(at, 128), :].astype(F32) * column).astype(BF16)

    own_meta.wait()
    meta_copies[0].wait()
    choose(0)

    for step in range(2):
        flip = step

        if step == 0:
            own_x.wait()
            x_copy.wait()

        def dispatch(k):
            dy, fxh = order(k)
            return remote(
                packed.at[k], arrived.at[step, core, k], d_send.at[k], d_recv.at[step, k],
                device(flip=flip, dy=dy, fxh=fxh),
            )

        for pair in range(0 if step == 0 else STREAM // 2, CHIPS // 2):
            sent = jnp.dot(
                pick[2 * pair : 2 * pair + 2].reshape(2 * block, 2 * rows), xb[step].reshape(2 * rows, half),
                preferred_element_type=F32,
            ).astype(BF16).reshape(2, block, half)
            for i in range(2):
                k = 2 * pair + i
                if step == 0 and k == OWN:
                    arrived[0, core, OWN] = sent[i]
                else:
                    packed[k] = sent[i]
                    dispatch(k).start()

        if step == 0:
            turn(0)
            gains = [gain_ref[0:1, j * 128 : (j + 1) * 128] for j in range(width // 128)]
            gain_t[...] = jnp.concatenate(gains + [jnp.zeros((128 - len(gains), 128), F32)], axis=0).T
            for copy in weight_copies:
                copy.wait()
            loop(0, width // 128, scale_weights)
            wd_copy.wait()
        else:
            all_sent(0)

        def forward(k, side):
            place = arrived.at[step, side, k]
            return remote(place, place, f_send.at[k], f_recv.at[step, k], partner)

        def share(g, at):
            place = hidden.at[
                step, pl.ds(pl.multiple_of(g * per * block, per * block), per * block), pl.ds(at, hid)
            ]
            return remote(place, place, h_send.at[g], h_recv.at[step, g], partner)

        def serve(g):
            for i in range(per):
                k = g * per + i
                if step == 0:

                    @pl.when(k != OWN)
                    def _():
                        dispatch(k).wait_recv()
                else:
                    dispatch(k).wait_recv()
                forward(k, core).start()
            for i in range(per):
                forward(g * per + i, other).wait_recv()
            both = [
                arrived[step, side, pl.ds(g * per, per)].reshape(per * block, half) for side in range(2)
            ]
            product = jnp.dot(both[0], wgu[0:half, :], preferred_element_type=F32)
            product = product + jnp.dot(both[1], wgu[half:width, :], preferred_element_type=F32)
            sums = jnp.zeros((per * block, 128), F32)
            for side in range(2):
                for i in range(half // 128):
                    piece = both[side][:, i * 128 : (i + 1) * 128].astype(F32)
                    sums = sums + piece * piece
            total = jnp.sum(sums, axis=-1, keepdims=True)
            product = product * lax.rsqrt(total * (1.0 / width) + 1e-06)
            value = (jax.nn.silu(product[:, 0:hid]) * product[:, hid:]).astype(BF16)
            hidden[step, pl.ds(pl.multiple_of(g * per * block, per * block), per * block), pl.ds(hid_at, hid)] = value
            share(g, hid_at).start()

        def give(q, k):
            dy, fxh = order(k)
            return remote(
                outgo.at[q, k], back.at[step, q, k], c_send.at[q, k], c_recv.at[step, q, k],
                device(flip=flip, dy=-dy, fxh=fxh),
            )

        def finish(q, first, count):
            value = jnp.dot(
                hidden[step, first * per * block : (first + count) * per * block, :],
                wdn[:, pl.ds(pl.multiple_of(q * cw, cw), cw)],
                preferred_element_type=F32,
            ).astype(BF16).reshape(count * per, block, cw)
            for i in range(count * per):
                k = first * per + i
                if step == 0 and k == OWN:
                    back[0, q, OWN] = value[i]
                else:
                    outgo[q, k] = value[i]
                    give(q, k).start()

        loop(0, GROUPS - 1, serve)
        loop(0, GROUPS - 1, lambda g: share(g, hid_there).wait_recv())
        loop(0, EARLY, lambda q: finish(q, 0, GROUPS - 1))
        serve(GROUPS - 1)
        share(GROUPS - 1, hid_there).wait_recv()
        loop(0, EARLY, lambda q: finish(q, GROUPS - 1, 1))
        loop(EARLY, CHUNKS, lambda q: finish(q, 0, GROUPS))

        if step == 0:
            meta_copies[1].wait()
            for copy in meta_copies[2:]:
                copy.wait_send()
            for part in range(2):
                remote(
                    meta_ref, meta1.at[part], m_send.at[2], m_recv.at[2 + part], device(flip=1, to=part)
                ).wait_recv()
            choose(1)
            turn(1)

            def dispatched(k):
                forward(k, core).wait_send()

                @pl.when(k != OWN)
                def _():
                    dispatch(k).wait_send()

            loop(0, CHIPS, dispatched)

        def relay(q):
            return remote(
                stage.at[0, q], xb.at[1, :, :, pl.ds(pl.multiple_of(q * cw, cw), cw)],
                r_send.at[q], r_recv.at[q], device(dz=1),
            )

        def hand(q, part, dz):
            columns = pl.ds(pl.multiple_of(core * half + q * cw, cw), cw)
            return remote(
                stage.at[1, q, part], o_ref.at[:, columns], o_send.at[q, part], o_recv.at[q, core],
                device(dz=dz, to=part),
            )

        def keep(q):
            columns = pl.ds(pl.multiple_of(core * half + q * cw, cw), cw)
            return pltpu.make_async_copy(stage.at[1, q, core], o_ref.at[:, columns], l_sem.at[3 + q])

        def combine(q):
            for k in range(CHIPS):
                if not (step == 0 and k == OWN):
                    give(q, k).wait_recv()
            at = pl.multiple_of(q * cw, cw)
            value = jnp.dot(
                pickt[step], back[step, q].reshape(CHIPS * block, cw), preferred_element_type=F32
            )
            for part in range(2):
                low = (2 + part) * rows
                new = (
                    xb[step, part, :, pl.ds(at, cw)].astype(F32)
                    + (value[part * rows : (part + 1) * rows] + value[low : low + rows])
                ).astype(BF16)
                stage[step, q, part] = new

            if step == 0:

                @pl.when(x_lo == 1)
                def _():
                    relay(q).start()

                @pl.when(x_lo == 0)
                def _():
                    xb[1, :, :, pl.ds(at, cw)] = stage[0, q]
            else:

                @pl.when(x_lo == 0)
                def _():
                    for part in range(2):
                        hand(q, part, 1).start()

                @pl.when(x_lo == 1)
                def _():
                    hand(q, other, 0).start()
                    keep(q).start()

        def stream(q):
            @pl.when(x_lo == 1)
            def _():
                relay(q).wait_recv()

            columns = pl.ds(pl.multiple_of(q * cw, cw), cw)
            sent = jnp.dot(
                pick[0:STREAM].reshape(STREAM * block, 2 * rows), xb[1, :, :, columns].reshape(2 * rows, cw),
                preferred_element_type=F32,
            ).astype(BF16).reshape(STREAM, block, cw)
            for k in range(STREAM):
                dy, fxh = order(k)
                packed[k, :, columns] = sent[k]
                remote(
                    packed.at[k, :, columns], arrived.at[1, core, k, :, columns], d_send.at[k], d_recv.at[1, k],
                    device(flip=1, dy=dy, fxh=fxh),
                ).start()

        if step == 0:

            def combine_and_stream(q):
                @pl.when(q < CHUNKS)
                def _():
                    combine(q)

                @pl.when(q >= LAG)
                def _():
                    stream(q - LAG)

            loop(0, CHUNKS + LAG, combine_and_stream)
        else:
            loop(0, CHUNKS, combine)


        def all_sent(done):
            def sent_all(k):
                if done == 0:

                    @pl.when(k != OWN)
                    def _():
                        loop(0, CHUNKS, lambda q: give(q, k).wait_send())
                else:
                    forward(k, core).wait_send()
                    dispatch(k).wait_send()
                    loop(0, CHUNKS, lambda q: give(q, k).wait_send())

            loop(0, CHIPS, sent_all)
            loop(0, GROUPS, lambda g: share(g, hid_at).wait_send())

        if step == 0:

            @pl.when(x_lo == 1)
            def _():
                loop(0, CHUNKS, lambda q: relay(q).wait_send())
        else:
            all_sent(1)

            @pl.when(x_lo == 0)
            def _():
                for part in range(2):
                    loop(0, CHUNKS, lambda q: hand(q, part, 1).wait_send())

            @pl.when(x_lo == 1)
            def _():
                loop(0, CHUNKS, lambda q: hand(q, other, 0).wait_send())
                loop(0, CHUNKS, lambda q: keep(q).wait())

            def taken(q, part):
                columns = pl.ds(pl.multiple_of(part * half + q * cw, cw), cw)
                remote(
                    stage.at[1, q, 0], o_ref.at[:, columns], o_send.at[q, 0], o_recv.at[q, part], partner
                ).wait_recv()

            @pl.when(x_lo == 0)
            def _():
                for part in range(2):
                    loop(0, CHUNKS, lambda q: taken(q, part))

            @pl.when(x_lo == 1)
            def _():
                loop(0, CHUNKS, lambda q: taken(q, other))


def body(state, lengths, gain, w_gate, w_up, w_down, expert_ids, gate_weights):
    rows, width = state.shape[1:]
    hid = w_gate.shape[2]
    half = width // 2
    block = 2 * CAP
    cw = half // CHUNKS
    meta = jnp.concatenate(
        [
            expert_ids[:, 0].transpose(0, 2, 1).reshape(4, rows).astype(F32),
            gate_weights[:, 0].transpose(0, 2, 1).reshape(4, rows),
            jnp.broadcast_to(lengths.astype(F32)[:, None], (8, rows)),
        ],
        axis=0,
    )
    vmem = pl.BlockSpec(memory_space=pltpu.VMEM)
    anywhere = pl.BlockSpec(memory_space=pl.ANY)
    dma = pltpu.SemaphoreType.DMA
    out = pl.pallas_call(
        kernel,
        out_shape=jax.ShapeDtypeStruct((rows, width), BF16),
        in_specs=[anywhere, vmem, vmem, anywhere, anywhere, anywhere],
        out_specs=anywhere,
        scratch_shapes=[
            pltpu.VMEM((2, 2, rows, half), BF16),
            pltpu.VMEM((2, 16, rows), F32),
            pltpu.VMEM((2, 16, rows), F32),
            pltpu.VMEM((16, rows), F32),
            pltpu.VMEM((128, 128), F32),
            pltpu.VMEM((width, 2 * hid), BF16),
            pltpu.VMEM((2 * hid, half), BF16),
            pltpu.VMEM((CHIPS, block, 2 * rows), BF16),
            pltpu.VMEM((CHIPS, block, 2 * rows), F32),
            pltpu.VMEM((2, 4 * rows, CHIPS * block), BF16),
            pltpu.VMEM((CHIPS, block, half), BF16),
            pltpu.VMEM((2, 2, CHIPS, block, half), BF16),
            pltpu.VMEM((2, CHIPS * block, 2 * hid), BF16),
            pltpu.VMEM((CHUNKS, CHIPS, block, cw), BF16),
            pltpu.VMEM((2, CHUNKS, CHIPS, block, cw), BF16),
            pltpu.VMEM((2, CHUNKS, 2, rows, cw), BF16),
            dma((3,)),
            dma, dma,
            dma, dma,
            dma((4,)), dma((4,)),
            dma((CHIPS,)), dma((2, CHIPS)),
            dma((CHIPS,)), dma((2, CHIPS)),
            dma((GROUPS,)), dma((2, GROUPS)),
            dma((CHUNKS, CHIPS)), dma((2, CHUNKS, CHIPS)),
            dma((CHUNKS,)), dma((CHUNKS,)),
            dma((CHUNKS, 2)), dma((CHUNKS, 2)),
            dma((3 + CHUNKS,)),
        ],
        compiler_params=pltpu.CompilerParams(
            collective_id=0, has_side_effects=True, vmem_limit_bytes=58 * 2**20
        ),
        cost_estimate=pl.CostEstimate(
            flops=2 * 2 * CHIPS * block * width * 3 * hid, bytes_accessed=3 * width * hid * 2 + 2 * rows * width * 2,
            transcendentals=0,
        ),
    )(state[0], meta, gain, w_gate[0], w_up[0], w_down[0])
    return out[None]


def solution(mesh):
    return jax.shard_map(
        body,
        mesh=mesh,
        in_specs=(
            P("section", "expert", None),
            P("section"),
            P("section", None),
            P("section", None, "expert"),
            P("section", None, "expert"),
            P("section", "expert", None),
            P(None, "section", "expert", None),
            P(None, "section", "expert", None),
        ),
        out_specs=P("section", "expert", None),
        check_vma=False,
    )
```

```python
import functools

import jax
import jax.numpy as jnp
from jax import lax
from jax.experimental import pallas as pl
from jax.experimental.pallas import tpu as pltpu
from jax.sharding import PartitionSpec as P

CAP = 40
CHIPS = 8
OWN = 2
CHUNKS = 8
GROUPS = 4
STREAM = 4
LAG = 1
EARLY = 2
MESH = pl.DeviceIdType.MESH
F32 = jnp.float32
BF16 = jnp.bfloat16


def order(k):
    m = k % 4
    return (2 * m + 1 - m // 2) % 4, (k % 2 + k // 4) % 2


def kernel(
    x_ref, meta_ref, gain_ref, wg_ref, wu_ref, wd_ref, o_ref,
    xb, meta0, meta1, metaz, gain_t, wgu, wdn, pick, pickw, pickt,
    packed, arrived, hidden, outgo, back, stage,
    w_sem, wd_send, wd_recv, x_send, x_recv, m_send, m_recv,
    d_send, d_recv, f_send, f_recv, h_send, h_recv, c_send, c_recv, r_send, r_recv, o_send, o_recv, l_sem,
):
    rows = x_ref.shape[0]
    width = x_ref.shape[1]
    half = width // 2
    hid = wg_ref.shape[1]
    block = 2 * CAP
    cw = half // CHUNKS
    per = CHIPS // GROUPS
    section = lax.axis_index("section")
    expert = lax.axis_index("expert")
    depth = lax.axis_size("section") // 2
    z = section // 2
    x_lo = section % 2
    y = expert // 4
    x_hi = (expert // 2) % 2
    core = expert % 2
    other = 1 - core
    chip = expert // 2

    def device(dz=0, flip=0, dy=0, fxh=0, to=None):
        to = core if to is None else to
        return (
            ((z + dz + depth) % depth) * 2 + (x_lo + flip) % 2,
            (((y + dy + 4) % 4) * 2 + (x_hi + fxh) % 2) * 2 + to,
        )

    partner = device(to=other)
    mine = pl.multiple_of(core * half, half)
    theirs = pl.multiple_of(other * half, half)

    def remote(src, dst, send, recv, to):
        return pltpu.make_async_remote_copy(
            src_ref=src, dst_ref=dst, send_sem=send, recv_sem=recv, device_id=to, device_id_type=MESH
        )

    def loop(first, last, step):
        lax.fori_loop(first, last, lambda i, c: (step(i), c)[1], 0)

    hid_at = pl.multiple_of(core * hid, hid)
    hid_there = pl.multiple_of(other * hid, hid)
    weight_copies = [
        pltpu.make_async_copy(wg_ref, wgu.at[:, pl.ds(0, hid)], w_sem.at[0]),
        pltpu.make_async_copy(wu_ref, wgu.at[:, pl.ds(hid, hid)], w_sem.at[1]),
        pltpu.make_async_copy(wd_ref.at[:, pl.ds(mine, half)], wdn.at[pl.ds(hid_at, hid), :], w_sem.at[2]),
    ]
    own_x = pltpu.make_async_copy(x_ref.at[:, pl.ds(mine, half)], xb.at[0, core], l_sem.at[0])
    own_meta = pltpu.make_async_copy(meta_ref, meta0.at[core], l_sem.at[2])
    own_x.start()
    own_meta.start()

    barrier = pltpu.get_barrier_semaphore()

    def greet(to):
        pl.semaphore_signal(barrier, inc=1, device_id=to, device_id_type=MESH)

    greet(partner)

    def greet_chips(k):
        dy, fxh = order(k)
        greet(device(flip=1, dy=dy, fxh=fxh))

        @pl.when(k != OWN)
        def _():
            greet(device(dy=dy, fxh=fxh))

    loop(0, CHIPS, greet_chips)
    greet(device(flip=1, to=other))
    for dz in (1, -1):
        for to in (core, other):
            greet(device(dz=dz, to=to))
    for copy in weight_copies:
        copy.start()
    pl.semaphore_wait(barrier, 2 * CHIPS + 5)

    x_copy = remote(x_ref.at[:, pl.ds(theirs, half)], xb.at[0, core], x_send, x_recv, partner)
    meta_copies = [
        remote(meta_ref, meta0.at[core], m_send.at[0], m_recv.at[0], partner),
        remote(meta_ref, metaz, m_send.at[1], m_recv.at[1], device(dz=1)),
        remote(meta_ref, meta1.at[core], m_send.at[2], m_recv.at[2 + core], device(flip=1, to=core)),
        remote(meta_ref, meta1.at[core], m_send.at[3], m_recv.at[2 + core], device(flip=1, to=other)),
    ]
    meta_copies[0].start()
    x_copy.start()
    for copy in meta_copies[1:]:
        copy.start()
    wd_copy = remote(
        wd_ref.at[:, pl.ds(theirs, half)], wdn.at[pl.ds(hid_at, hid), :], wd_send, wd_recv, partner
    )
    wd_copy.start()

    sub8 = lax.broadcasted_iota(jnp.int32, (8, rows), 0).astype(F32)
    before = (
        lax.broadcasted_iota(jnp.int32, (rows, rows), 0) < lax.broadcasted_iota(jnp.int32, (rows, rows), 1)
    ).astype(BF16)
    lane = lax.broadcasted_iota(jnp.int32, (1, rows), 1)
    slot_no = lax.broadcasted_iota(jnp.int32, (block, rows), 0).astype(F32)

    def choose(step):
        meta = meta1 if step else meta0
        choices = []
        for part in range(2):
            if step == 0:
                length = meta0[part, 8:9, :]
            else:
                length = jnp.where(x_lo == 0, meta0[0, 8:9, :], metaz[8:9, :])
            live = ((chip * 2 + part) * rows + lane).astype(F32) < length
            ids = [meta[part, 2 * step + k : 2 * step + k + 1, :] for k in range(2)]
            gates = [meta[part, 4 + 2 * step + k : 5 + 2 * step + k, :] for k in range(2)]
            ones = [jnp.where((i == sub8) & live, 1.0, 0.0) for i in ids]
            earlier = jnp.dot((ones[0] + ones[1]).astype(BF16), before, preferred_element_type=F32)
            slots = [
                jnp.where(live, jnp.sum(earlier * one, axis=0, keepdims=True) + float(part * CAP), -1.0)
                for one in ones
            ]
            choices.append((ids, gates, slots))

        def match_chip(k):
            dy, fxh = order(k)
            target = (((y + dy) % 4) * 2 + (x_hi + fxh) % 2).astype(F32)
            hits, weighted = [], []
            for ids, gates, slots in choices:
                match = [jnp.where((ids[i] == target) & (slots[i] == slot_no), 1.0, 0.0) for i in range(2)]
                hits.append(match[0] + match[1])
                weighted.append(match[0] * gates[0] + match[1] * gates[1])
            pick[k] = jnp.concatenate(hits, axis=1).astype(BF16)
            pickw[k] = jnp.concatenate(weighted, axis=1)

        loop(0, CHIPS, match_chip)

    def turn(step):
        turned = pickw[...].reshape(CHIPS * block, 2 * rows).T
        high = turned.astype(BF16)
        pickt[step, 0 : 2 * rows] = high
        pickt[step, 2 * rows :] = (turned - high.astype(F32)).astype(BF16)

    def scale_weights(j):
        at = pl.multiple_of(j * 128, 128)
        column = jnp.sum(
            jnp.where(lax.broadcasted_iota(jnp.int32, (128, 128), 1) == j, gain_t[...], 0.0), axis=1, keepdims=True
        )
        wgu[pl.ds(at, 128), :] = (wgu[pl.ds(at, 128), :].astype(F32) * column).astype(BF16)

    own_meta.wait()
    meta_copies[0].wait()
    choose(0)

    for step in range(2):
        flip = step

        if step == 0:
            own_x.wait()
            x_copy.wait()

        def dispatch(k):
            dy, fxh = order(k)
            return remote(
                packed.at[k], arrived.at[step, core, k], d_send.at[k], d_recv.at[step, k],
                device(flip=flip, dy=dy, fxh=fxh),
            )

        def pack(first, q, step=step):
            columns = pl.ds(pl.multiple_of(q * cw, cw), cw)
            sent = jnp.dot(
                pick[first : first + STREAM].reshape(STREAM * block, 2 * rows),
                xb[step, :, :, columns].reshape(2 * rows, cw), preferred_element_type=F32,
            ).astype(BF16).reshape(STREAM, block, cw)
            for i in range(STREAM):
                k = first + i
                if step == 0 and k == OWN:
                    arrived[0, core, OWN, :, columns] = sent[i]
                    continue
                dy, fxh = order(k)
                packed[k, :, columns] = sent[i]
                remote(
                    packed.at[k, :, columns], arrived.at[step, core, k, :, columns], d_send.at[k], d_recv.at[step, k],
                    device(flip=step, dy=dy, fxh=fxh),
                ).start()

        for first in range(0 if step == 0 else STREAM, CHIPS, STREAM):
            loop(0, CHUNKS, lambda q: pack(first, q))

        if step == 0:
            turn(0)
            gains = [gain_ref[0:1, j * 128 : (j + 1) * 128] for j in range(width // 128)]
            gain_t[...] = jnp.concatenate(gains + [jnp.zeros((128 - len(gains), 128), F32)], axis=0).T
            for copy in weight_copies:
                copy.wait()
            loop(0, width // 128, scale_weights)
            wd_copy.wait()
        else:
            all_sent(0)

        def forward(k, side):
            place = arrived.at[step, side, k]
            return remote(place, place, f_send.at[k], f_recv.at[step, k], partner)

        def share(g, at):
            place = hidden.at[
                step, pl.ds(pl.multiple_of(g * per * block, per * block), per * block), pl.ds(at, hid)
            ]
            return remote(place, place, h_send.at[g], h_recv.at[step, g], partner)

        def serve(g):
            for i in range(per):
                k = g * per + i
                if step == 0:

                    @pl.when(k != OWN)
                    def _():
                        dispatch(k).wait_recv()
                else:
                    dispatch(k).wait_recv()
                forward(k, core).start()
            for i in range(per):
                forward(g * per + i, other).wait_recv()
            both = [
                arrived[step, side, pl.ds(g * per, per)].reshape(per * block, half) for side in range(2)
            ]
            product = jnp.dot(both[0], wgu[0:half, :], preferred_element_type=F32)
            product = product + jnp.dot(both[1], wgu[half:width, :], preferred_element_type=F32)
            sums = jnp.zeros((per * block, 128), F32)
            for side in range(2):
                for i in range(half // 128):
                    piece = both[side][:, i * 128 : (i + 1) * 128].astype(F32)
                    sums = sums + piece * piece
            total = jnp.sum(sums, axis=-1, keepdims=True)
            product = product * lax.rsqrt(total * (1.0 / width) + 1e-06)
            value = (jax.nn.silu(product[:, 0:hid]) * product[:, hid:]).astype(BF16)
            hidden[step, pl.ds(pl.multiple_of(g * per * block, per * block), per * block), pl.ds(hid_at, hid)] = value
            share(g, hid_at).start()

        def give(q, k):
            dy, fxh = order(k)
            return remote(
                outgo.at[q, k], back.at[step, q, k], c_send.at[q, k], c_recv.at[step, q, k],
                device(flip=flip, dy=-dy, fxh=fxh),
            )

        def finish(q, first, count):
            value = jnp.dot(
                hidden[step, first * per * block : (first + count) * per * block, :],
                wdn[:, pl.ds(pl.multiple_of(q * cw, cw), cw)],
                preferred_element_type=F32,
            ).astype(BF16).reshape(count * per, block, cw)
            for i in range(count * per):
                k = first * per + i
                if step == 0 and k == OWN:
                    back[0, q, OWN] = value[i]
                else:
                    outgo[q, k] = value[i]
                    give(q, k).start()

        loop(0, GROUPS - 1, serve)
        loop(0, GROUPS - 1, lambda g: share(g, hid_there).wait_recv())
        loop(0, EARLY, lambda q: finish(q, 0, GROUPS - 1))
        serve(GROUPS - 1)
        share(GROUPS - 1, hid_there).wait_recv()
        loop(0, EARLY, lambda q: finish(q, GROUPS - 1, 1))
        loop(EARLY, CHUNKS, lambda q: finish(q, 0, GROUPS))

        if step == 0:
            meta_copies[1].wait()
            for copy in meta_copies[2:]:
                copy.wait_send()
            for part in range(2):
                remote(
                    meta_ref, meta1.at[part], m_send.at[2], m_recv.at[2 + part], device(flip=1, to=part)
                ).wait_recv()
            choose(1)
            turn(1)

            def dispatched(k):
                forward(k, core).wait_send()

                @pl.when(k != OWN)
                def _():
                    dispatch(k).wait_send()

            loop(0, CHIPS, dispatched)

        def relay(q):
            return remote(
                stage.at[0, q], xb.at[1, :, :, pl.ds(pl.multiple_of(q * cw, cw), cw)],
                r_send.at[q], r_recv.at[q], device(dz=1),
            )

        def hand(q, part, dz):
            columns = pl.ds(pl.multiple_of(core * half + q * cw, cw), cw)
            return remote(
                stage.at[1, q, part], o_ref.at[:, columns], o_send.at[q, part], o_recv.at[q, core],
                device(dz=dz, to=part),
            )

        def keep(q):
            columns = pl.ds(pl.multiple_of(core * half + q * cw, cw), cw)
            return pltpu.make_async_copy(stage.at[1, q, core], o_ref.at[:, columns], l_sem.at[3 + q])

        def combine(q):
            for k in range(CHIPS):
                if not (step == 0 and k == OWN):
                    give(q, k).wait_recv()
            at = pl.multiple_of(q * cw, cw)
            value = jnp.dot(
                pickt[step], back[step, q].reshape(CHIPS * block, cw), preferred_element_type=F32
            )
            for part in range(2):
                low = (2 + part) * rows
                new = (
                    xb[step, part, :, pl.ds(at, cw)].astype(F32)
                    + (value[part * rows : (part + 1) * rows] + value[low : low + rows])
                ).astype(BF16)
                stage[step, q, part] = new

            if step == 0:

                @pl.when(x_lo == 1)
                def _():
                    relay(q).start()

                @pl.when(x_lo == 0)
                def _():
                    xb[1, :, :, pl.ds(at, cw)] = stage[0, q]
            else:

                @pl.when(x_lo == 0)
                def _():
                    for part in range(2):
                        hand(q, part, 1).start()

                @pl.when(x_lo == 1)
                def _():
                    hand(q, other, 0).start()
                    keep(q).start()

        def stream(q):
            @pl.when(x_lo == 1)
            def _():
                relay(q).wait_recv()

            pack(0, q, 1)

        if step == 0:

            def combine_and_stream(q):
                @pl.when(q < CHUNKS)
                def _():
                    combine(q)

                @pl.when(q >= LAG)
                def _():
                    stream(q - LAG)

            loop(0, CHUNKS + LAG, combine_and_stream)
        else:
            loop(0, CHUNKS, combine)


        def all_sent(done):
            def sent_all(k):
                if done == 0:

                    @pl.when(k != OWN)
                    def _():
                        loop(0, CHUNKS, lambda q: give(q, k).wait_send())
                else:
                    forward(k, core).wait_send()
                    dispatch(k).wait_send()
                    loop(0, CHUNKS, lambda q: give(q, k).wait_send())

            loop(0, CHIPS, sent_all)
            loop(0, GROUPS, lambda g: share(g, hid_at).wait_send())

        if step == 0:

            @pl.when(x_lo == 1)
            def _():
                loop(0, CHUNKS, lambda q: relay(q).wait_send())
        else:
            all_sent(1)

            @pl.when(x_lo == 0)
            def _():
                for part in range(2):
                    loop(0, CHUNKS, lambda q: hand(q, part, 1).wait_send())

            @pl.when(x_lo == 1)
            def _():
                loop(0, CHUNKS, lambda q: hand(q, other, 0).wait_send())
                loop(0, CHUNKS, lambda q: keep(q).wait())

            def taken(q, part):
                columns = pl.ds(pl.multiple_of(part * half + q * cw, cw), cw)
                remote(
                    stage.at[1, q, 0], o_ref.at[:, columns], o_send.at[q, 0], o_recv.at[q, part], partner
                ).wait_recv()

            @pl.when(x_lo == 0)
            def _():
                for part in range(2):
                    loop(0, CHUNKS, lambda q: taken(q, part))

            @pl.when(x_lo == 1)
            def _():
                loop(0, CHUNKS, lambda q: taken(q, other))


def body(state, lengths, gain, w_gate, w_up, w_down, expert_ids, gate_weights):
    rows, width = state.shape[1:]
    hid = w_gate.shape[2]
    half = width // 2
    block = 2 * CAP
    cw = half // CHUNKS
    meta = jnp.concatenate(
        [
            expert_ids[:, 0].transpose(0, 2, 1).reshape(4, rows).astype(F32),
            gate_weights[:, 0].transpose(0, 2, 1).reshape(4, rows),
            jnp.broadcast_to(lengths.astype(F32)[:, None], (8, rows)),
        ],
        axis=0,
    )
    vmem = pl.BlockSpec(memory_space=pltpu.VMEM)
    anywhere = pl.BlockSpec(memory_space=pl.ANY)
    dma = pltpu.SemaphoreType.DMA
    out = pl.pallas_call(
        kernel,
        out_shape=jax.ShapeDtypeStruct((rows, width), BF16),
        in_specs=[anywhere, vmem, vmem, anywhere, anywhere, anywhere],
        out_specs=anywhere,
        scratch_shapes=[
            pltpu.VMEM((2, 2, rows, half), BF16),
            pltpu.VMEM((2, 16, rows), F32),
            pltpu.VMEM((2, 16, rows), F32),
            pltpu.VMEM((16, rows), F32),
            pltpu.VMEM((128, 128), F32),
            pltpu.VMEM((width, 2 * hid), BF16),
            pltpu.VMEM((2 * hid, half), BF16),
            pltpu.VMEM((CHIPS, block, 2 * rows), BF16),
            pltpu.VMEM((CHIPS, block, 2 * rows), F32),
            pltpu.VMEM((2, 4 * rows, CHIPS * block), BF16),
            pltpu.VMEM((CHIPS, block, half), BF16),
            pltpu.VMEM((2, 2, CHIPS, block, half), BF16),
            pltpu.VMEM((2, CHIPS * block, 2 * hid), BF16),
            pltpu.VMEM((CHUNKS, CHIPS, block, cw), BF16),
            pltpu.VMEM((2, CHUNKS, CHIPS, block, cw), BF16),
            pltpu.VMEM((2, CHUNKS, 2, rows, cw), BF16),
            dma((3,)),
            dma, dma,
            dma, dma,
            dma((4,)), dma((4,)),
            dma((CHIPS,)), dma((2, CHIPS)),
            dma((CHIPS,)), dma((2, CHIPS)),
            dma((GROUPS,)), dma((2, GROUPS)),
            dma((CHUNKS, CHIPS)), dma((2, CHUNKS, CHIPS)),
            dma((CHUNKS,)), dma((CHUNKS,)),
            dma((CHUNKS, 2)), dma((CHUNKS, 2)),
            dma((3 + CHUNKS,)),
        ],
        compiler_params=pltpu.CompilerParams(
            collective_id=0, has_side_effects=True, vmem_limit_bytes=58 * 2**20
        ),
        cost_estimate=pl.CostEstimate(
            flops=2 * 2 * CHIPS * block * width * 3 * hid, bytes_accessed=3 * width * hid * 2 + 2 * rows * width * 2,
            transcendentals=0,
        ),
    )(state[0], meta, gain, w_gate[0], w_up[0], w_down[0])
    return out[None]


def solution(mesh):
    return jax.shard_map(
        body,
        mesh=mesh,
        in_specs=(
            P("section", "expert", None),
            P("section"),
            P("section", None),
            P("section", None, "expert"),
            P("section", None, "expert"),
            P("section", "expert", None),
            P(None, "section", "expert", None),
            P(None, "section", "expert", None),
        ),
        out_specs=P("section", "expert", None),
        check_vma=False,
    )
```

```python
import functools

import jax
import jax.numpy as jnp
from jax import lax
from jax.experimental import pallas as pl
from jax.experimental.pallas import tpu as pltpu
from jax.sharding import PartitionSpec as P

CAP = 40
CHIPS = 8
OWN = 2
CHUNKS = 8
GROUPS = 2
STREAM = 4
LAG = 1
EARLY = 2
MESH = pl.DeviceIdType.MESH
F32 = jnp.float32
BF16 = jnp.bfloat16


def order(k):
    m = k % 4
    return (2 * m + 1 - m // 2) % 4, (k % 2 + k // 4) % 2


def kernel(
    x_ref, meta_ref, gain_ref, wg_ref, wu_ref, wd_ref, o_ref,
    xb, meta0, meta1, metaz, gain_t, wgu, wdn, pick, pickw, pickt,
    packed, arrived, hidden, outgo, back, stage,
    w_sem, wd_send, wd_recv, x_send, x_recv, m_send, m_recv,
    d_send, d_recv, f_send, f_recv, h_send, h_recv, c_send, c_recv, r_send, r_recv, o_send, o_recv, l_sem,
):
    rows = x_ref.shape[0]
    width = x_ref.shape[1]
    half = width // 2
    hid = wg_ref.shape[1]
    block = 2 * CAP
    cw = half // CHUNKS
    per = CHIPS // GROUPS
    section = lax.axis_index("section")
    expert = lax.axis_index("expert")
    depth = lax.axis_size("section") // 2
    z = section // 2
    x_lo = section % 2
    y = expert // 4
    x_hi = (expert // 2) % 2
    core = expert % 2
    other = 1 - core
    chip = expert // 2

    def device(dz=0, flip=0, dy=0, fxh=0, to=None):
        to = core if to is None else to
        return (
            ((z + dz + depth) % depth) * 2 + (x_lo + flip) % 2,
            (((y + dy + 4) % 4) * 2 + (x_hi + fxh) % 2) * 2 + to,
        )

    partner = device(to=other)
    mine = pl.multiple_of(core * half, half)
    theirs = pl.multiple_of(other * half, half)

    def remote(src, dst, send, recv, to):
        return pltpu.make_async_remote_copy(
            src_ref=src, dst_ref=dst, send_sem=send, recv_sem=recv, device_id=to, device_id_type=MESH
        )

    def loop(first, last, step):
        lax.fori_loop(first, last, lambda i, c: (step(i), c)[1], 0)

    hid_at = pl.multiple_of(core * hid, hid)
    hid_there = pl.multiple_of(other * hid, hid)
    weight_copies = [
        pltpu.make_async_copy(wg_ref, wgu.at[:, pl.ds(0, hid)], w_sem.at[0]),
        pltpu.make_async_copy(wu_ref, wgu.at[:, pl.ds(hid, hid)], w_sem.at[1]),
        pltpu.make_async_copy(wd_ref.at[:, pl.ds(mine, half)], wdn.at[pl.ds(hid_at, hid), :], w_sem.at[2]),
    ]
    own_x = pltpu.make_async_copy(x_ref.at[:, pl.ds(mine, half)], xb.at[0, core], l_sem.at[0])
    own_meta = pltpu.make_async_copy(meta_ref, meta0.at[core], l_sem.at[2])
    own_x.start()
    own_meta.start()

    barrier = pltpu.get_barrier_semaphore()

    def greet(to):
        pl.semaphore_signal(barrier, inc=1, device_id=to, device_id_type=MESH)

    greet(partner)

    def greet_chips(k):
        dy, fxh = order(k)
        greet(device(flip=1, dy=dy, fxh=fxh))

        @pl.when(k != OWN)
        def _():
            greet(device(dy=dy, fxh=fxh))

    loop(0, CHIPS, greet_chips)
    greet(device(flip=1, to=other))
    for dz in (1, -1):
        for to in (core, other):
            greet(device(dz=dz, to=to))
    for copy in weight_copies:
        copy.start()
    pl.semaphore_wait(barrier, 2 * CHIPS + 5)

    x_copy = remote(x_ref.at[:, pl.ds(theirs, half)], xb.at[0, core], x_send, x_recv, partner)
    meta_copies = [
        remote(meta_ref, meta0.at[core], m_send.at[0], m_recv.at[0], partner),
        remote(meta_ref, metaz, m_send.at[1], m_recv.at[1], device(dz=1)),
        remote(meta_ref, meta1.at[core], m_send.at[2], m_recv.at[2 + core], device(flip=1, to=core)),
        remote(meta_ref, meta1.at[core], m_send.at[3], m_recv.at[2 + core], device(flip=1, to=other)),
    ]
    meta_copies[0].start()
    x_copy.start()
    for copy in meta_copies[1:]:
        copy.start()
    wd_copy = remote(
        wd_ref.at[:, pl.ds(theirs, half)], wdn.at[pl.ds(hid_at, hid), :], wd_send, wd_recv, partner
    )
    wd_copy.start()

    sub8 = lax.broadcasted_iota(jnp.int32, (8, rows), 0).astype(F32)
    before = (
        lax.broadcasted_iota(jnp.int32, (rows, rows), 0) < lax.broadcasted_iota(jnp.int32, (rows, rows), 1)
    ).astype(BF16)
    lane = lax.broadcasted_iota(jnp.int32, (1, rows), 1)
    slot_no = lax.broadcasted_iota(jnp.int32, (block, rows), 0).astype(F32)

    def choose(step):
        meta = meta1 if step else meta0
        choices = []
        for part in range(2):
            if step == 0:
                length = meta0[part, 8:9, :]
            else:
                length = jnp.where(x_lo == 0, meta0[0, 8:9, :], metaz[8:9, :])
            live = ((chip * 2 + part) * rows + lane).astype(F32) < length
            ids = [meta[part, 2 * step + k : 2 * step + k + 1, :] for k in range(2)]
            gates = [meta[part, 4 + 2 * step + k : 5 + 2 * step + k, :] for k in range(2)]
            ones = [jnp.where((i == sub8) & live, 1.0, 0.0) for i in ids]
            earlier = jnp.dot((ones[0] + ones[1]).astype(BF16), before, preferred_element_type=F32)
            slots = [
                jnp.where(live, jnp.sum(earlier * one, axis=0, keepdims=True) + float(part * CAP), -1.0)
                for one in ones
            ]
            choices.append((ids, gates, slots))

        def match_chip(k):
            dy, fxh = order(k)
            target = (((y + dy) % 4) * 2 + (x_hi + fxh) % 2).astype(F32)
            hits, weighted = [], []
            for ids, gates, slots in choices:
                match = [jnp.where((ids[i] == target) & (slots[i] == slot_no), 1.0, 0.0) for i in range(2)]
                hits.append(match[0] + match[1])
                weighted.append(match[0] * gates[0] + match[1] * gates[1])
            pick[k] = jnp.concatenate(hits, axis=1).astype(BF16)
            pickw[k] = jnp.concatenate(weighted, axis=1)

        loop(0, CHIPS, match_chip)

    def turn(step):
        turned = pickw[...].reshape(CHIPS * block, 2 * rows).T
        high = turned.astype(BF16)
        pickt[step, 0 : 2 * rows] = high
        pickt[step, 2 * rows :] = (turned - high.astype(F32)).astype(BF16)

    def scale_weights(j):
        at = pl.multiple_of(j * 128, 128)
        column = jnp.sum(
            jnp.where(lax.broadcasted_iota(jnp.int32, (128, 128), 1) == j, gain_t[...], 0.0), axis=1, keepdims=True
        )
        wgu[pl.ds(at, 128), :] = (wgu[pl.ds(at, 128), :].astype(F32) * column).astype(BF16)

    own_meta.wait()
    meta_copies[0].wait()
    choose(0)

    for step in range(2):
        flip = step

        if step == 0:
            own_x.wait()
            x_copy.wait()

        def dispatch(k):
            dy, fxh = order(k)
            return remote(
                packed.at[k], arrived.at[step, core, k], d_send.at[k], d_recv.at[step, k],
                device(flip=flip, dy=dy, fxh=fxh),
            )

        def pack(first, q, step=step):
            columns = pl.ds(pl.multiple_of(q * cw, cw), cw)
            sent = jnp.dot(
                pick[first : first + STREAM].reshape(STREAM * block, 2 * rows),
                xb[step, :, :, columns].reshape(2 * rows, cw), preferred_element_type=F32,
            ).astype(BF16).reshape(STREAM, block, cw)
            for i in range(STREAM):
                k = first + i
                if step == 0 and k == OWN:
                    arrived[0, core, OWN, :, columns] = sent[i]
                    continue
                dy, fxh = order(k)
                packed[k, :, columns] = sent[i]
                remote(
                    packed.at[k, :, columns], arrived.at[step, core, k, :, columns], d_send.at[k], d_recv.at[step, k],
                    device(flip=step, dy=dy, fxh=fxh),
                ).start()

        for first in range(0 if step == 0 else STREAM, CHIPS, STREAM):
            loop(0, CHUNKS, lambda q: pack(first, q))

        if step == 0:
            turn(0)
            gains = [gain_ref[0:1, j * 128 : (j + 1) * 128] for j in range(width // 128)]
            gain_t[...] = jnp.concatenate(gains + [jnp.zeros((128 - len(gains), 128), F32)], axis=0).T
            for copy in weight_copies:
                copy.wait()
            loop(0, width // 128, scale_weights)
            wd_copy.wait()
        else:
            all_sent(0)

        def forward(k, side):
            place = arrived.at[step, side, k]
            return remote(place, place, f_send.at[k], f_recv.at[step, k], partner)

        def share(g, at):
            place = hidden.at[
                step, pl.ds(pl.multiple_of(g * per * block, per * block), per * block), pl.ds(at, hid)
            ]
            return remote(place, place, h_send.at[g], h_recv.at[step, g], partner)

        def serve(g):
            for i in range(per):
                k = g * per + i
                if step == 0:

                    @pl.when(k != OWN)
                    def _():
                        dispatch(k).wait_recv()
                else:
                    dispatch(k).wait_recv()
                forward(k, core).start()
            for i in range(per):
                forward(g * per + i, other).wait_recv()
            both = [
                arrived[step, side, pl.ds(g * per, per)].reshape(per * block, half) for side in range(2)
            ]
            product = jnp.dot(both[0], wgu[0:half, :], preferred_element_type=F32)
            product = product + jnp.dot(both[1], wgu[half:width, :], preferred_element_type=F32)
            sums = jnp.zeros((per * block, 128), F32)
            for side in range(2):
                for i in range(half // 128):
                    piece = both[side][:, i * 128 : (i + 1) * 128].astype(F32)
                    sums = sums + piece * piece
            total = jnp.sum(sums, axis=-1, keepdims=True)
            product = product * lax.rsqrt(total * (1.0 / width) + 1e-06)
            value = (jax.nn.silu(product[:, 0:hid]) * product[:, hid:]).astype(BF16)
            hidden[step, pl.ds(pl.multiple_of(g * per * block, per * block), per * block), pl.ds(hid_at, hid)] = value
            share(g, hid_at).start()

        def give(q, k):
            dy, fxh = order(k)
            return remote(
                outgo.at[q, k], back.at[step, q, k], c_send.at[q, k], c_recv.at[step, q, k],
                device(flip=flip, dy=-dy, fxh=fxh),
            )

        def finish(q, first, count):
            value = jnp.dot(
                hidden[step, first * per * block : (first + count) * per * block, :],
                wdn[:, pl.ds(pl.multiple_of(q * cw, cw), cw)],
                preferred_element_type=F32,
            ).astype(BF16).reshape(count * per, block, cw)
            for i in range(count * per):
                k = first * per + i
                if step == 0 and k == OWN:
                    back[0, q, OWN] = value[i]
                else:
                    outgo[q, k] = value[i]
                    give(q, k).start()

        loop(0, GROUPS - 1, serve)
        loop(0, GROUPS - 1, lambda g: share(g, hid_there).wait_recv())
        loop(0, EARLY, lambda q: finish(q, 0, GROUPS - 1))
        serve(GROUPS - 1)
        share(GROUPS - 1, hid_there).wait_recv()
        loop(0, EARLY, lambda q: finish(q, GROUPS - 1, 1))
        loop(EARLY, CHUNKS, lambda q: finish(q, 0, GROUPS))

        if step == 0:
            meta_copies[1].wait()
            for copy in meta_copies[2:]:
                copy.wait_send()
            for part in range(2):
                remote(
                    meta_ref, meta1.at[part], m_send.at[2], m_recv.at[2 + part], device(flip=1, to=part)
                ).wait_recv()
            choose(1)
            turn(1)

            def dispatched(k):
                forward(k, core).wait_send()

                @pl.when(k != OWN)
                def _():
                    dispatch(k).wait_send()

            loop(0, CHIPS, dispatched)

        def relay(q):
            return remote(
                stage.at[0, q], xb.at[1, :, :, pl.ds(pl.multiple_of(q * cw, cw), cw)],
                r_send.at[q], r_recv.at[q], device(dz=1),
            )

        def hand(q, part, dz):
            columns = pl.ds(pl.multiple_of(core * half + q * cw, cw), cw)
            return remote(
                stage.at[1, q, part], o_ref.at[:, columns], o_send.at[q, part], o_recv.at[q, core],
                device(dz=dz, to=part),
            )

        def keep(q):
            columns = pl.ds(pl.multiple_of(core * half + q * cw, cw), cw)
            return pltpu.make_async_copy(stage.at[1, q, core], o_ref.at[:, columns], l_sem.at[3 + q])

        def combine(q):
            for k in range(CHIPS):
                if not (step == 0 and k == OWN):
                    give(q, k).wait_recv()
            at = pl.multiple_of(q * cw, cw)
            value = jnp.dot(
                pickt[step], back[step, q].reshape(CHIPS * block, cw), preferred_element_type=F32
            )
            for part in range(2):
                low = (2 + part) * rows
                new = (
                    xb[step, part, :, pl.ds(at, cw)].astype(F32)
                    + (value[part * rows : (part + 1) * rows] + value[low : low + rows])
                ).astype(BF16)
                stage[step, q, part] = new

            if step == 0:

                @pl.when(x_lo == 1)
                def _():
                    relay(q).start()

                @pl.when(x_lo == 0)
                def _():
                    xb[1, :, :, pl.ds(at, cw)] = stage[0, q]
            else:

                @pl.when(x_lo == 0)
                def _():
                    for part in range(2):
                        hand(q, part, 1).start()

                @pl.when(x_lo == 1)
                def _():
                    hand(q, other, 0).start()
                    keep(q).start()

        def stream(q):
            @pl.when(x_lo == 1)
            def _():
                relay(q).wait_recv()

            pack(0, q, 1)

        if step == 0:

            def combine_and_stream(q):
                @pl.when(q < CHUNKS)
                def _():
                    combine(q)

                @pl.when(q >= LAG)
                def _():
                    stream(q - LAG)

            loop(0, CHUNKS + LAG, combine_and_stream)
        else:
            loop(0, CHUNKS, combine)


        def all_sent(done):
            def sent_all(k):
                if done == 0:

                    @pl.when(k != OWN)
                    def _():
                        loop(0, CHUNKS, lambda q: give(q, k).wait_send())
                else:
                    forward(k, core).wait_send()
                    dispatch(k).wait_send()
                    loop(0, CHUNKS, lambda q: give(q, k).wait_send())

            loop(0, CHIPS, sent_all)
            loop(0, GROUPS, lambda g: share(g, hid_at).wait_send())

        if step == 0:

            @pl.when(x_lo == 1)
            def _():
                loop(0, CHUNKS, lambda q: relay(q).wait_send())
        else:
            all_sent(1)

            @pl.when(x_lo == 0)
            def _():
                for part in range(2):
                    loop(0, CHUNKS, lambda q: hand(q, part, 1).wait_send())

            @pl.when(x_lo == 1)
            def _():
                loop(0, CHUNKS, lambda q: hand(q, other, 0).wait_send())
                loop(0, CHUNKS, lambda q: keep(q).wait())

            def taken(q, part):
                columns = pl.ds(pl.multiple_of(part * half + q * cw, cw), cw)
                remote(
                    stage.at[1, q, 0], o_ref.at[:, columns], o_send.at[q, 0], o_recv.at[q, part], partner
                ).wait_recv()

            @pl.when(x_lo == 0)
            def _():
                for part in range(2):
                    loop(0, CHUNKS, lambda q: taken(q, part))

            @pl.when(x_lo == 1)
            def _():
                loop(0, CHUNKS, lambda q: taken(q, other))


def body(state, lengths, gain, w_gate, w_up, w_down, expert_ids, gate_weights):
    rows, width = state.shape[1:]
    hid = w_gate.shape[2]
    half = width // 2
    block = 2 * CAP
    cw = half // CHUNKS
    meta = jnp.concatenate(
        [
            expert_ids[:, 0].transpose(0, 2, 1).reshape(4, rows).astype(F32),
            gate_weights[:, 0].transpose(0, 2, 1).reshape(4, rows),
            jnp.broadcast_to(lengths.astype(F32)[:, None], (8, rows)),
        ],
        axis=0,
    )
    vmem = pl.BlockSpec(memory_space=pltpu.VMEM)
    anywhere = pl.BlockSpec(memory_space=pl.ANY)
    dma = pltpu.SemaphoreType.DMA
    out = pl.pallas_call(
        kernel,
        out_shape=jax.ShapeDtypeStruct((rows, width), BF16),
        in_specs=[anywhere, vmem, vmem, anywhere, anywhere, anywhere],
        out_specs=anywhere,
        scratch_shapes=[
            pltpu.VMEM((2, 2, rows, half), BF16),
            pltpu.VMEM((2, 16, rows), F32),
            pltpu.VMEM((2, 16, rows), F32),
            pltpu.VMEM((16, rows), F32),
            pltpu.VMEM((128, 128), F32),
            pltpu.VMEM((width, 2 * hid), BF16),
            pltpu.VMEM((2 * hid, half), BF16),
            pltpu.VMEM((CHIPS, block, 2 * rows), BF16),
            pltpu.VMEM((CHIPS, block, 2 * rows), F32),
            pltpu.VMEM((2, 4 * rows, CHIPS * block), BF16),
            pltpu.VMEM((CHIPS, block, half), BF16),
            pltpu.VMEM((2, 2, CHIPS, block, half), BF16),
            pltpu.VMEM((2, CHIPS * block, 2 * hid), BF16),
            pltpu.VMEM((CHUNKS, CHIPS, block, cw), BF16),
            pltpu.VMEM((2, CHUNKS, CHIPS, block, cw), BF16),
            pltpu.VMEM((2, CHUNKS, 2, rows, cw), BF16),
            dma((3,)),
            dma, dma,
            dma, dma,
            dma((4,)), dma((4,)),
            dma((CHIPS,)), dma((2, CHIPS)),
            dma((CHIPS,)), dma((2, CHIPS)),
            dma((GROUPS,)), dma((2, GROUPS)),
            dma((CHUNKS, CHIPS)), dma((2, CHUNKS, CHIPS)),
            dma((CHUNKS,)), dma((CHUNKS,)),
            dma((CHUNKS, 2)), dma((CHUNKS, 2)),
            dma((3 + CHUNKS,)),
        ],
        compiler_params=pltpu.CompilerParams(
            collective_id=0, has_side_effects=True, vmem_limit_bytes=58 * 2**20
        ),
        cost_estimate=pl.CostEstimate(
            flops=2 * 2 * CHIPS * block * width * 3 * hid, bytes_accessed=3 * width * hid * 2 + 2 * rows * width * 2,
            transcendentals=0,
        ),
    )(state[0], meta, gain, w_gate[0], w_up[0], w_down[0])
    return out[None]


def solution(mesh):
    return jax.shard_map(
        body,
        mesh=mesh,
        in_specs=(
            P("section", "expert", None),
            P("section"),
            P("section", None),
            P("section", None, "expert"),
            P("section", None, "expert"),
            P("section", "expert", None),
            P(None, "section", "expert", None),
            P(None, "section", "expert", None),
        ),
        out_specs=P("section", "expert", None),
        check_vma=False,
    )
```
